512 devices in a mesh: dom: 128 (over y, z, core), phase: 4 (over x).
Axes of the slice: x: 4, y: 8, z: 8, core: 2. Of those that a mesh axis runs over, the one named last changes fastest.
Arguments:
- grid_in: bfloat16 [4, 131072, 474], P('phase', 'dom'), may hold values from -6 to 6
- mesh_static: bfloat16 [32768, 512], P('dom'), may hold values from -6 to 6
- embed_w: bfloat16 [474, 512], P(None, 'phase'), may hold values from -0.25 to 0.25
- grid_w: bfloat16 [512, 512], P(None, 'phase'), may hold values from -0.25 to 0.25
- enc_w: bfloat16 [512, 512], P(None, 'phase'), may hold values from -0.25 to 0.25
- src_w: bfloat16 [2, 512, 512], P(None, None, 'phase'), may hold values from -0.25 to 0.25
- node_w: bfloat16 [2, 512, 512], P(None, None, 'phase'), may hold values from -0.25 to 0.25
- dec_w: bfloat16 [512, 512], P(None, 'phase'), may hold values from -0.25 to 0.25
- out_w: bfloat16 [512, 227], P('phase'), may hold values from -0.25 to 0.25
- cotangent: bfloat16 [4, 131072, 227], P('phase', 'dom'), may hold values from -6 to 6
- grid_send: int32 [128, 6, 12], P('dom'), may hold values from 0 to 1023
- g2m_src: int32 [128, 2048], P('dom'), may hold values from 0 to 1095, as said below
- g2m_dst: int32 [128, 2048], P('dom'), may hold values from 0 to 255, never falling along the last dimension, each value on 1 to 24 neighbouring positions
- mesh_send: int32 [128, 6, 8], P('dom'), may hold values from 0 to 255
- mesh_src: int32 [128, 2048], P('dom'), may hold values from 0 to 303, as said below
- mesh_dst: int32 [128, 2048], P('dom'), may hold values from 0 to 255, never falling along the last dimension, each value on 1 to 24 neighbouring positions
- dec_send: int32 [128, 6, 8], P('dom'), may hold values from 0 to 255
- m2g_src: int32 [128, 3072], P('dom'), may hold values from 0 to 303, as said below
- m2g_dst: int32 [128, 3072], P('dom'), may hold values from 0 to 1023, never falling along the last dimension, each value on 1 to 8 neighbouring positions
Outputs:
- pred: bfloat16 [4, 131072, 227], P('phase', 'dom')
- input_grad: bfloat16 [4, 131072, 474], P('phase', 'dom')
The draws below stay inside these ranges and needn't reach their ends.
Inputs may be any that keep to these rules, and one draw needn't show every extreme that they name: `g2m_src`: on partition d, entries below 1024 name own grid rows; every slot entry 1024 + k * 12 + s is named by exactly one edge of d. `mesh_src`: on partition d, entries below 256 name own mesh rows; every slot entry is named by exactly one edge of d. `m2g_src`: on partition d, entries below 256 name own mesh rows; every slot entry is named by exactly one edge of d.
All inputs are finite; a program needn't handle non-finite values.
Results may differ from the reference program's by a relative error of at most 0.02.
Values may be sent and summed in bfloat16 or wider, within the bound.
No kernel may reach another device: no remote copies, remote signals or barrier semaphores. Data moves between devices by JAX's collectives and lax.ppermute only.
A program may use at most 128 MiB of HBM per device.

```python
import math
import jax
import jax.numpy as jnp
import numpy as np
from jax import lax

D = 512
F_IN = 474
F_OUT = 227
GRID_DEV = 1024
LAYERS = 2
NEIGHBOURS = 6
GRID_SLOT = 12
MESH_SLOT = 8
DEC_SLOT = 8
MESH_DEV = 256
G2M_DEV = 2048
MESH_EDGES_DEV = 2048
M2G_DEV = 3072
SAMPLES = 4
GRID = 131072
MESH = 32768
N_DOM = 128


def edge_sources(key, local_count, halo_count, edge_count):
    device_keys = jax.random.split(key, N_DOM)

    def one_device(device_key):
        pick_key, order_key = jax.random.split(device_key)
        own_rows = jax.random.randint(pick_key, (edge_count - halo_count,), 0, local_count, dtype=jnp.int32)
        received = local_count + jnp.arange(halo_count, dtype=jnp.int32)
        return jax.random.permutation(order_key, jnp.concatenate([received, own_rows]))
    return jax.vmap(one_device)(device_keys).astype(jnp.int32)


def draw_g2m_src(key, part):
    key = jax.random.fold_in(key, 11)
    return edge_sources(key, GRID_DEV, NEIGHBOURS * GRID_SLOT, G2M_DEV)


def draw_mesh_src(key, part):
    key = jax.random.fold_in(key, 23)
    return edge_sources(key, MESH_DEV, NEIGHBOURS * MESH_SLOT, MESH_EDGES_DEV)


def draw_m2g_src(key, part):
    key = jax.random.fold_in(key, 37)
    return edge_sources(key, MESH_DEV, NEIGHBOURS * DEC_SLOT, M2G_DEV)


def with_ends(values, own_key, smallest, high):
    spot = [jax.random.randint(jax.random.fold_in(own_key, axis), (), 0, length) for axis, length in enumerate(values.shape)]
    longest = values.shape.index(max(values.shape))
    beside = spot[:longest] + [(spot[longest] + 1) % values.shape[longest]] + spot[longest + 1:]
    return values.at[tuple(spot)].set(smallest).at[tuple(beside)].set(high)


def levels(stream_key, extent, cuts, least, largest):
    def one(dim, blocks):
        steps = jax.random.uniform(jax.random.fold_in(jax.random.fold_in(stream_key, 6), dim), (blocks,), jnp.float32, least / len(cuts), largest / len(cuts))
        return jnp.repeat(jnp.exp(steps), extent[dim] // blocks).reshape((-1,) + (1,) * (len(extent) - dim - 1))

    factor_of = one(*cuts[0])
    for cut in cuts[1:]:
        factor_of = factor_of * one(*cut)
    return factor_of


def profile(count, total, limit, skew):
    weights = [(1 << 20) // math.isqrt(standing ** skew) + 1 for standing in range(2, count + 1)]
    surplus, given = total - limit - (count - 1), [1] * (count - 1)
    while surplus > 0:
        free = [i for i in range(count - 1) if given[i] < limit]
        whole, left = sum([weights[i] for i in free]), surplus
        for i in free:
            more = min(limit - given[i], max(1, left * weights[i] // whole), surplus)
            given[i] = given[i] + more
            surplus = surplus - more
    return np.array([limit] + given)


def uneven_parts(own_key, count, total, reach, skew):
    if count == 2:
        one = jax.random.randint(own_key, (), max(1, total - reach), min(reach, total - 1) + 1)
        return jnp.stack([one, total - one])
    sizes = jnp.asarray(profile(count, total, reach, skew), jnp.int32)
    twos = (count - 1) // 2
    source_of, sink = sizes[1:1 + 2 * twos:2], sizes[2:2 + 2 * twos:2]
    slack = jnp.minimum(source_of - 1, reach - sink)
    moved = jax.random.randint(jax.random.fold_in(own_key, 1), (twos,), 0, 1 << 20) % (slack + 1)
    sizes = sizes.at[1:1 + 2 * twos:2].set(source_of - moved).at[2:2 + 2 * twos:2].set(sink + moved)
    return sizes[jax.random.permutation(jax.random.fold_in(own_key, 2), count)]


def normal_values(stream_key, shape, deviation, reach, shards=(), kind=jnp.bfloat16):
    array = jax.random.normal(stream_key, shape, jnp.float32) * deviation
    if len(shards) > 0:
        array = levels(stream_key, shape, shards, -0.22, 0.18) * array
    return jnp.clip(array, min=-reach, max=reach).astype(kind)


def setup_inputs(seed: int = 0) -> dict:
    keys = jax.random.split(jax.random.key(seed), 20)
    return {
        "grid_in": normal_values(keys[0], (SAMPLES, GRID, F_IN), 1.0, 6.0, ((0, 4), (1, 128))),
        "mesh_static": normal_values(keys[1], (MESH, D), 1.0, 6.0, ((0, 128),)),
        "embed_w": normal_values(keys[2], (F_IN, D), F_IN ** -0.5, 0.25, ((1, 4),)),
        "grid_w": normal_values(keys[3], (D, D), D ** -0.5, 0.25, ((1, 4),)),
        "enc_w": normal_values(keys[4], (D, D), D ** -0.5, 0.25, ((1, 4),)),
        "src_w": normal_values(keys[5], (LAYERS, D, D), D ** -0.5, 0.25, ((2, 4),)),
        "node_w": normal_values(keys[6], (LAYERS, D, D), D ** -0.5, 0.25, ((2, 4),)),
        "dec_w": normal_values(keys[7], (D, D), D ** -0.5, 0.25, ((1, 4),)),
        "out_w": normal_values(keys[8], (D, F_OUT), D ** -0.5, 0.25, ((0, 4),)),
        "cotangent": normal_values(keys[9], (SAMPLES, GRID, F_OUT), 1.0, 6.0, ((0, 4), (1, 128))),
        "grid_send": with_ends(jax.random.randint(keys[10], (N_DOM, NEIGHBOURS, GRID_SLOT), 0, GRID_DEV), jax.random.fold_in(keys[10], 1), 0, GRID_DEV - 1).astype(jnp.int32),
        "g2m_src": draw_g2m_src(jax.random.fold_in(keys[19], 71), 0),
        "g2m_dst": jax.vmap(lambda own: jnp.searchsorted(jnp.cumsum(uneven_parts(own, MESH_DEV, G2M_DEV, 24, 2)), jnp.arange(G2M_DEV), side="right"))(jax.random.split(keys[12], N_DOM)).reshape((N_DOM, G2M_DEV)).astype(jnp.int32),
        "mesh_send": with_ends(jax.random.randint(keys[13], (N_DOM, NEIGHBOURS, MESH_SLOT), 0, MESH_DEV), jax.random.fold_in(keys[13], 1), 0, MESH_DEV - 1).astype(jnp.int32),
        "mesh_src": draw_mesh_src(jax.random.fold_in(keys[19], 71), 0),
        "mesh_dst": jax.vmap(lambda own: jnp.searchsorted(jnp.cumsum(uneven_parts(own, MESH_DEV, MESH_EDGES_DEV, 24, 2)), jnp.arange(MESH_EDGES_DEV), side="right"))(jax.random.split(keys[15], N_DOM)).reshape((N_DOM, MESH_EDGES_DEV)).astype(jnp.int32),
        "dec_send": with_ends(jax.random.randint(keys[16], (N_DOM, NEIGHBOURS, DEC_SLOT), 0, MESH_DEV), jax.random.fold_in(keys[16], 1), 0, MESH_DEV - 1).astype(jnp.int32),
        "m2g_src": draw_m2g_src(jax.random.fold_in(keys[19], 71), 0),
        "m2g_dst": jax.vmap(lambda own: jnp.searchsorted(jnp.cumsum(uneven_parts(own, GRID_DEV, M2G_DEV, 8, 2)), jnp.arange(M2G_DEV), side="right"))(jax.random.split(keys[18], N_DOM)).reshape((N_DOM, M2G_DEV)).astype(jnp.int32),
    }


EPSILON = 1e-06

def bfloat(values):
    return values.astype(jnp.bfloat16)

def single(values):
    return values.astype(jnp.float32)

def silu_slope(values):
    sigmoid_value = jax.nn.sigmoid(values)
    return sigmoid_value * (1.0 + values * (1.0 - sigmoid_value))

def inverse_rms(values):
    return lax.rsqrt(lax.optimization_barrier(jnp.mean(values * values, axis=-1, keepdims=True)) + EPSILON)

def forward_product(left, right):
    return jnp.dot(left, right, preferred_element_type=jnp.float32)

def backward_product(left, right):
    return lax.dot_general(left, right, (((1,), (1,)), ((), ())), preferred_element_type=jnp.float32)

def neighbour_offsets(count):
    position = jnp.arange(count, dtype=jnp.int32)
    return ((position // 2 + 1) * (1 - 2 * (position % 2))).astype(jnp.int32)

def source_rows(sources, send_table, local_count, slot_count):
    devices = sources.shape[0]
    owners = jnp.arange(devices, dtype=jnp.int32)[:, None]
    offsets = neighbour_offsets(send_table.shape[1])
    offset = jnp.maximum(sources - local_count, 0)
    groups = offset // slot_count
    within = offset % slot_count
    peers = (owners - offsets[groups]) % devices
    remote = peers * local_count + send_table[peers, groups, within]
    return jnp.where(sources < local_count, owners * local_count + sources, remote).reshape(-1).astype(jnp.int32)

def entry_rows(sources, local_count, halo_count):
    devices = sources.shape[0]
    span = local_count + halo_count
    owners = jnp.arange(devices, dtype=jnp.int32)[:, None]
    return (owners * span + sources).reshape(-1).astype(jnp.int32)

def receiver_rows(receivers, local_count):
    devices = receivers.shape[0]
    owners = jnp.arange(devices, dtype=jnp.int32)[:, None]
    return (owners * local_count + receivers).reshape(-1).astype(jnp.int32)

def return_rule(edge_grad, entries, send_table, local_count):
    devices, neighbours, slot_count = send_table.shape
    features = edge_grad.shape[-1]
    span = local_count + neighbours * slot_count
    entry_sums = bfloat(jax.ops.segment_sum(single(edge_grad), entries, num_segments=devices * span))
    blocks = entry_sums.reshape(devices, span, features)
    own_rows = single(blocks[:, :local_count].reshape(-1, features))
    halo_rows = single(blocks[:, local_count:].reshape(-1, features))
    owners = jnp.arange(devices, dtype=jnp.int32)[:, None, None]
    groups = jnp.arange(neighbours, dtype=jnp.int32)[None, :, None]
    slots = jnp.arange(slot_count, dtype=jnp.int32)[None, None, :]
    offsets = neighbour_offsets(neighbours)[None, :, None]
    peers = (owners - offsets) % devices
    targets = (peers * local_count + send_table[peers, groups, slots]).reshape(-1).astype(jnp.int32)
    return bfloat(own_rows + jax.ops.segment_sum(halo_rows, targets, num_segments=devices * local_count))

def reference(grid_in, mesh_static, embed_w, grid_w, enc_w, src_w, node_w, dec_w, out_w, cotangent, grid_send, g2m_src, g2m_dst, mesh_send, mesh_src, mesh_dst, dec_send, m2g_src, m2g_dst):
    grid_total = GRID_DEV * N_DOM
    mesh_total = MESH_DEV * N_DOM
    grid_source = source_rows(g2m_src, grid_send, GRID_DEV, GRID_SLOT)
    grid_entry = entry_rows(g2m_src, GRID_DEV, NEIGHBOURS * GRID_SLOT)
    grid_receiver = receiver_rows(g2m_dst, MESH_DEV)
    mesh_source = source_rows(mesh_src, mesh_send, MESH_DEV, MESH_SLOT)
    mesh_entry = entry_rows(mesh_src, MESH_DEV, NEIGHBOURS * MESH_SLOT)
    mesh_receiver = receiver_rows(mesh_dst, MESH_DEV)
    dec_source = source_rows(m2g_src, dec_send, MESH_DEV, DEC_SLOT)
    dec_entry = entry_rows(m2g_src, MESH_DEV, NEIGHBOURS * DEC_SLOT)
    dec_receiver = receiver_rows(m2g_dst, GRID_DEV)

    def one_sample(sample_pair):
        grid_rows, cotangent_rows = sample_pair
        pre_hidden = forward_product(grid_rows, embed_w)
        hidden = bfloat(jax.nn.silu(pre_hidden))
        projected = bfloat(forward_product(hidden, grid_w))
        enc_pre = single(projected[grid_source]) + single(mesh_static[grid_receiver])
        enc_msg = bfloat(jax.nn.silu(enc_pre))
        enc_sum = bfloat(jax.ops.segment_sum(single(enc_msg), grid_receiver, num_segments=mesh_total, indices_are_sorted=True))
        encoded = forward_product(enc_sum, enc_w)
        enc_scale = inverse_rms(encoded)
        latent = bfloat(single(mesh_static) + encoded * enc_scale)
        stored = []
        for layer_index in range(LAYERS):
            src_proj = bfloat(forward_product(latent, src_w[layer_index]))
            edge_pre = single(src_proj[mesh_source]) + single(latent[mesh_receiver])
            edge_msg = bfloat(jax.nn.silu(edge_pre))
            edge_sum = bfloat(jax.ops.segment_sum(single(edge_msg), mesh_receiver, num_segments=mesh_total, indices_are_sorted=True))
            update = forward_product(edge_sum, node_w[layer_index])
            layer_scale = inverse_rms(update)
            stored.append((edge_pre, update, layer_scale))
            latent = bfloat(single(latent) + update * layer_scale)
        decoded = bfloat(forward_product(latent, dec_w))
        dec_pre = single(decoded[dec_source]) + single(hidden[dec_receiver])
        dec_msg = bfloat(jax.nn.silu(dec_pre))
        dec_sum = bfloat(jax.ops.segment_sum(single(dec_msg), dec_receiver, num_segments=grid_total, indices_are_sorted=True))
        prediction = bfloat(forward_product(dec_sum, out_w))
        dec_sum_grad = bfloat(backward_product(cotangent_rows, out_w))
        dec_edge_grad = bfloat(single(dec_sum_grad[dec_receiver]) * silu_slope(dec_pre))
        decoded_grad = return_rule(dec_edge_grad, dec_entry, dec_send, MESH_DEV)
        latent_grad = backward_product(decoded_grad, dec_w)
        for layer_index in reversed(range(LAYERS)):
            edge_pre, update, layer_scale = stored[layer_index]
            mixed = lax.optimization_barrier(jnp.mean(latent_grad * update, axis=-1, keepdims=True))
            update_grad = bfloat(layer_scale * latent_grad - update * layer_scale ** 3 * mixed)
            sum_grad = bfloat(backward_product(update_grad, node_w[layer_index]))
            edge_grad = bfloat(single(sum_grad[mesh_receiver]) * silu_slope(edge_pre))
            src_grad = return_rule(edge_grad, mesh_entry, mesh_send, MESH_DEV)
            into_rows = jax.ops.segment_sum(single(edge_grad), mesh_receiver, num_segments=mesh_total, indices_are_sorted=True)
            latent_grad = latent_grad + into_rows + backward_product(src_grad, src_w[layer_index])
        mixed = lax.optimization_barrier(jnp.mean(latent_grad * encoded, axis=-1, keepdims=True))
        encoded_grad = bfloat(enc_scale * latent_grad - encoded * enc_scale ** 3 * mixed)
        summed_grad = bfloat(backward_product(encoded_grad, enc_w))
        msg_grad = bfloat(single(summed_grad[grid_receiver]) * silu_slope(enc_pre))
        projected_grad = return_rule(msg_grad, grid_entry, grid_send, GRID_DEV)
        skip_grad = jax.ops.segment_sum(single(dec_edge_grad), dec_receiver, num_segments=grid_total, indices_are_sorted=True)
        hidden_grad = backward_product(projected_grad, grid_w) + skip_grad
        pre_grad = bfloat(hidden_grad * silu_slope(pre_hidden))
        input_gradient = bfloat(backward_product(pre_grad, embed_w))
        return (prediction, input_gradient)
    predictions, gradients = lax.map(one_sample, (grid_in, cotangent))
    return (predictions, gradients)
```

```python
import functools

import jax
import jax.numpy as jnp
import numpy as np
from jax import lax
from jax.experimental import pallas as pl
from jax.experimental.pallas import tpu as pltpu
from jax.sharding import PartitionSpec as P

EPSILON = 1e-06
LANES = 128
BF = jnp.bfloat16
F32 = jnp.float32
EVEN = (0, 4, 1, 5, 2, 3)
ODD = (1, 0, 5, 4, 2, 3)
SWAP = (0, 2, 1, 3, 5, 4)
NEIGHBOURS = 6
BLOCK = 256
HALF = 128


def shape(rows, columns, dtype=BF):
    return jax.ShapeDtypeStruct((rows, columns), dtype)


def call(body, outs, args, flops, scratch=(), small=None):
    vmem = pl.BlockSpec(memory_space=pltpu.VMEM)
    smem = pl.BlockSpec(memory_space=pltpu.SMEM)
    moved = sum(a.size * a.dtype.itemsize for a in args)
    moved += sum(o.size * jnp.dtype(o.dtype).itemsize for o in outs)
    return pl.pallas_call(
        body,
        out_shape=tuple(outs),
        in_specs=[smem if i == small else vmem for i in range(len(args))],
        out_specs=tuple([vmem] * len(outs)),
        scratch_shapes=list(scratch),
        compiler_params=pltpu.CompilerParams(vmem_limit_bytes=48 << 20),
        cost_estimate=pl.CostEstimate(flops=flops, bytes_accessed=moved, transcendentals=0),
    )(*args)


def mm(left, right):
    return jnp.dot(left, right, preferred_element_type=F32)


def mm_back(left, right):
    return lax.dot_general(left, right, (((1,), (1,)), ((), ())), preferred_element_type=F32)


def gate(values):
    return 0.5 * jnp.tanh(0.5 * values) + 0.5


def gate_slope(values, sigmoid):
    return sigmoid * (1.0 + values * (1.0 - sigmoid))


def column(row):
    return jnp.broadcast_to(row, (LANES, row.shape[1])).T


def pick(col, count):
    lane = lax.broadcasted_iota(jnp.int32, col.shape, 1)
    tiles = [
        jnp.where(lane + LANES * t == col, 1.0, 0.0).astype(BF) for t in range(count // LANES)
    ]
    return tiles[0] if len(tiles) == 1 else jnp.concatenate(tiles, axis=1)


def spread(row, count):
    own = lax.broadcasted_iota(jnp.int32, (count, row.shape[1]), 0)
    return jnp.where(own == row, 1.0, 0.0).astype(BF)


def weight(ref, start, rows):
    return jnp.concatenate([ref[j, start : start + rows, :] for j in range(ref.shape[0])], axis=1)


def stack_rows(refs):
    rows = jnp.concatenate([r[...].astype(F32) for r in refs], axis=0)
    short = LANES - rows.shape[0]
    return jnp.concatenate([rows, jnp.zeros((short, rows.shape[1]), F32)], axis=0).astype(BF)


def put_rows(refs, rows):
    each = refs[0].shape[0]
    for k, ref in enumerate(refs):
        ref[...] = rows[k * each : (k + 1) * each, :].astype(BF)


def inverse_rms(values):
    return lax.rsqrt(jnp.mean(values * values, axis=-1, keepdims=True) + EPSILON)


def norm_grad(grad, update, scale):
    mixed = jnp.mean(grad * update, axis=-1, keepdims=True)
    return (scale * grad - update * (scale * scale * scale) * mixed).astype(BF)


def prepare_kernel(gs, gd, ms, md, ds, dd, entries, tables, grid_in, cotangent, cols, rows, *sends):
    lists = ((gs, gd), (ms, md), (ds, dd))
    for which, (src, dst) in enumerate(lists):
        blocks, width = src.shape
        slots = column(entries[which : which + 1, :])
        entry = jnp.concatenate([slots] * (width // LANES), axis=1)
        found = jnp.zeros((LANES, width), F32)
        for b in range(blocks):
            dst_row = jnp.broadcast_to(dst[b : b + 1, :], (LANES, width)).astype(F32)
            found += jnp.where(entry == src[b : b + 1, :], dst_row, 0.0)
        total = jnp.sum(found, axis=1, keepdims=True)
        wide = jnp.broadcast_to(total, (LANES, LANES)).astype(jnp.int32)
        wide = jnp.where(slots >= 0, wide, -1)
        cols[which] = wide
        rows[which] = wide.T
    for t in range(3):
        wide = jnp.broadcast_to(tables[t : t + 1, :], (LANES, LANES))
        rows[3 + t] = wide
        cols[3 + t] = wide.T
    sent = mm(pick(cols[3], grid_in.shape[0]), grid_in[...])
    at = pick(cols[2], grid_in.shape[0])
    back = mm(at, grid_in[...])
    back_cot = mm(at, cotangent[...])
    pad_in = jnp.zeros((8, 512 - grid_in.shape[1]), F32)
    pad_cot = jnp.zeros((8, 512 - cotangent.shape[1]), F32)
    for k in range(NEIGHBOURS):
        j = SWAP[k]
        first = jnp.concatenate([sent[16 * k : 16 * k + 8], pad_in], axis=1)
        second = jnp.concatenate([sent[16 * k + 8 : 16 * k + 16], pad_in], axis=1)
        third = jnp.concatenate([back[8 * j : 8 * j + 8], pad_in], axis=1)
        fourth = jnp.concatenate([back_cot[8 * j : 8 * j + 8], pad_cot], axis=1)
        sends[k][...] = jnp.concatenate([first, second, third, fourth], axis=0).astype(BF)


def embed_kernel(grid_in, cotangent, w, *refs):
    early = refs[:NEIGHBOURS]
    slope, hidden, ext, own_grad, b_hidden, b_grad = refs[NEIGHBOURS:]
    rows, f_in = grid_in.shape
    f_out = cotangent.shape[1]
    embed = weight(w, 0, f_in)
    mix = weight(w, 480, 512)
    halves = [[w[j, r : r + LANES, :] for j in range(4)] for r in (992, 992 + LANES)]
    out = jnp.concatenate([jnp.concatenate(h, axis=0) for h in halves], axis=1)[:, :f_out]
    received = [r[...].astype(F32) for r in early]

    def gathered(start, count, order, width):
        parts = [received[k][start : start + count, :width] for k in order]
        short = LANES - count * len(parts)
        return jnp.concatenate(parts + [jnp.zeros((short, width), F32)], axis=0).astype(BF)

    halo = gathered(0, 16, range(6), f_in)
    back = gathered(16, 8, SWAP, f_in)
    back_cot = gathered(24, 8, SWAP, f_out)
    pre = mm(halo, embed)
    ext[rows:, :] = mm((pre * gate(pre)).astype(BF), mix).astype(BF)
    pre = mm(back, embed)
    b_hidden[...] = (pre * gate(pre)).astype(BF)
    b_grad[...] = mm_back(back_cot, out).astype(BF)

    @pl.loop(0, rows // BLOCK)
    def _(b):
        at = pl.ds(pl.multiple_of(b * BLOCK, BLOCK), BLOCK)
        pre = mm(grid_in[at, :], embed)
        sig = gate(pre)
        slope[at, :] = gate_slope(pre, sig).astype(BF)
        own = (pre * sig).astype(BF)
        hidden[at, :] = own
        ext[at, :] = mm(own, mix).astype(BF)
        own_grad[at, :] = mm_back(cotangent[at, :], out).astype(BF)


def encode_kernel(ext, static, src, moves, dst, cols, w, *refs):
    slope, h_slope, encoded, scale, latent, proj = refs[:6]
    sends = refs[6:12]
    total = refs[12]
    count = ext.shape[0]
    meshes = static.shape[0]
    total[...] = jnp.zeros_like(total)

    @pl.loop(0, src.shape[0])
    def _(b):
        at = pl.ds(pl.multiple_of(b * BLOCK, BLOCK), BLOCK)
        dst_row = dst[pl.ds(b, 1), :]
        src_row = src[pl.ds(b, 1), :]
        for k in range(NEIGHBOURS):
            src_row += jnp.where(src[pl.ds(b, 1), :] >= count - LANES + 12 * k, moves[k], 0)
        pre = mm(pick(column(src_row), count), ext[...])
        pre += mm(pick(column(dst_row), meshes), static[...])
        sig = gate(pre)
        slope[at, :] = gate_slope(pre, sig).astype(BF)
        total[...] += mm(spread(dst_row, meshes), (pre * sig).astype(BF))

    pre = ext[count - LANES :, :].astype(F32) + mm(pick(cols[0], meshes), static[...])
    h_slope[...] = gate_slope(pre, gate(pre)).astype(BF)
    made = mm(total[...].astype(BF), weight(w, 0, 512))
    inverse = inverse_rms(made)
    encoded[...] = made
    scale[...] = jnp.broadcast_to(inverse, scale.shape)
    start = (static[...].astype(F32) + made * inverse).astype(BF)
    latent[...] = start
    sent = mm(start, weight(w, 512, 512)).astype(BF)
    proj[...] = sent
    put_rows(sends, mm(pick(cols[4], meshes), sent))


def edges_kernel(proj, latent, src, dst, total, slope):
    count = proj.shape[0]
    total[...] = jnp.zeros_like(total)

    @pl.loop(0, src.shape[0])
    def _(b):
        at = pl.ds(pl.multiple_of(b * BLOCK, BLOCK), BLOCK)
        dst_row = dst[pl.ds(b, 1), :]
        src_row = src[pl.ds(b, 1), :]
        pre = mm(pick(column(src_row), count), proj[...])
        pre += mm(pick(column(dst_row), count), latent[...])
        sig = gate(pre)
        slope[at, :] = gate_slope(pre, sig).astype(BF)
        own_row = jnp.where(src_row < count, dst_row, -1)
        total[...] += mm(spread(own_row, count), (pre * sig).astype(BF))


def layer_kernel(total, latent, cols, rows, w, *refs, last, starts):
    halo = refs[:NEIGHBOURS]
    h_slope, update, scale, new, proj = refs[NEIGHBOURS : NEIGHBOURS + 5]
    sends = refs[NEIGHBOURS + 5 :]
    count = latent.shape[0]
    old = latent[...]
    pre = stack_rows(halo).astype(F32) + mm(pick(cols[1], count), old)
    sig = gate(pre)
    h_slope[...] = gate_slope(pre, sig).astype(BF)
    summed = total[...] + mm(spread(rows[1][0:1, :], count), (pre * sig).astype(BF))
    made = mm(summed.astype(BF), weight(w, starts[0], 512))
    inverse = inverse_rms(made)
    update[...] = made
    scale[...] = jnp.broadcast_to(inverse, scale.shape)
    after = (old.astype(F32) + made * inverse).astype(BF)
    new[...] = after
    sent = mm(after, weight(w, starts[1], 512)).astype(BF)
    proj[...] = sent
    if not last:
        put_rows(sends, mm(pick(cols[4], count), sent))


def outgoing_grad(grad, cols, h_slope, count):
    return (mm(pick(cols, count), grad) * h_slope[...].astype(F32)).astype(BF)


def decode_kernel(proj, hidden, own_grad, b_hidden, b_grad, starts, src, dst, cols, rows, dec_w, node_w, update, scale, h_slope, *refs, where):
    messages, grads, latent_grad, sum_grad = refs[:4]
    sends = refs[4:10]
    entry = refs[10]
    count = proj.shape[0]
    entry[...] = jnp.zeros_like(entry)

    @pl.loop(0, src.shape[0])
    def _(b):
        at = pl.ds(pl.multiple_of(b * BLOCK, BLOCK), BLOCK)
        src_row = src[pl.ds(b, 1), :]
        dst_row = dst[pl.ds(b, 1), :]
        pre = mm(pick(column(src_row), count), proj[...])
        near, grad = [], []
        for half in range(BLOCK // HALF):
            start = pl.multiple_of(starts[2 * b + half], 16)
            window = pl.ds(start, BLOCK)
            local = column(dst_row[:, half * HALF : (half + 1) * HALF] - start)
            chosen = pick(local, BLOCK)
            near.append(mm(chosen, hidden[window, :]))
            grad.append(mm(chosen, own_grad[window, :]))
        pre += jnp.concatenate(near, axis=0)
        sig = gate(pre)
        messages[at, :] = (pre * sig).astype(BF)
        edge = (jnp.concatenate(grad, axis=0) * gate_slope(pre, sig)).astype(BF)
        grads[at, :] = edge
        entry[...] += mm(spread(src_row, count), edge)

    sent = mm(pick(cols[5], count), proj[...])
    pre = sent + b_hidden[...].astype(F32)
    far = (b_grad[...].astype(F32) * gate_slope(pre, gate(pre))).astype(BF)
    own = entry[...].astype(BF).astype(F32)
    row_grad = (own + mm(spread(rows[5][0:1, :], count), far)).astype(BF)
    grad = mm_back(row_grad, weight(dec_w, where[0], 512))
    latent_grad[...] = grad
    step = norm_grad(grad, update[...], scale[:, 0:1])
    back = mm_back(step, weight(node_w, where[1], 512)).astype(BF)
    sum_grad[...] = back
    out = outgoing_grad(back, cols[1], h_slope, count).astype(F32)
    for k in range(NEIGHBOURS):
        j = SWAP[k]
        both = jnp.concatenate([sent[8 * k : 8 * k + 8], out[8 * j : 8 * j + 8]], axis=0)
        sends[k][...] = both.astype(BF)


def predict_kernel(messages, grads, hidden, own_grad, starts, src, dst, cols, rows, w, *refs):
    halo = refs[:NEIGHBOURS]
    pred, skip = refs[NEIGHBOURS : NEIGHBOURS + 2]
    total = refs[NEIGHBOURS + 2]
    count, features = hidden.shape
    f_out = pred.shape[1]
    halves = [[w[j, r : r + LANES, :] for j in range(4)] for r in (992, 992 + LANES)]
    out = jnp.concatenate([jnp.concatenate(h, axis=0) for h in halves], axis=1)[:, :f_out]
    near = pick(cols[2], count)
    got = jnp.concatenate([r[...].astype(F32)[:8] for r in halo] + [jnp.zeros((80, features), F32)], axis=0)
    pre = got + mm(near, hidden[...])
    sig = gate(pre)
    place = spread(rows[2][0:1, :], count)
    total[...] = mm(place, (pre * sig).astype(BF))
    skip[...] = mm(place, (mm(near, own_grad[...]) * gate_slope(pre, sig)).astype(BF))

    @pl.loop(0, src.shape[0])
    def _(b):
        src_row = src[pl.ds(b, 1), :]
        dst_row = jnp.where(src_row < 256, dst[pl.ds(b, 1), :], -(1 << 20))
        for half in range(BLOCK // HALF):
            at = pl.ds(pl.multiple_of(b * BLOCK + half * HALF, HALF), HALF)
            start = pl.multiple_of(starts[2 * b + half], 16)
            window = pl.ds(start, BLOCK)
            chosen = spread(dst_row[:, half * HALF : (half + 1) * HALF] - start, BLOCK)
            total[window, :] += mm(chosen, messages[at, :])
            skip[window, :] += mm(chosen, grads[at, :])

    @pl.loop(0, count // BLOCK)
    def _(b):
        at = pl.ds(pl.multiple_of(b * BLOCK, BLOCK), BLOCK)
        pred[at, :] = mm(total[at, :].astype(BF), out).astype(BF)


def edges_back_kernel(sum_grad, slope, src, dst, rows, *refs):
    far = refs[:NEIGHBOURS]
    entry, into = refs[NEIGHBOURS : NEIGHBOURS + 2]
    acc = refs[NEIGHBOURS + 2]
    count = sum_grad.shape[0]
    keep = far[0].shape[0] - 8
    order = SWAP if keep else range(NEIGHBOURS)
    parts = [far[k][...].astype(F32)[keep:] for k in order]
    short = jnp.zeros((LANES - 8 * NEIGHBOURS, sum_grad.shape[1]), F32)
    outside = jnp.concatenate(parts + [short], axis=0).astype(BF)
    acc[...] = jnp.zeros_like(acc)
    into[...] = mm(spread(rows[1][0:1, :], count), outside)

    @pl.loop(0, src.shape[0])
    def _(b):
        at = pl.ds(pl.multiple_of(b * BLOCK, BLOCK), BLOCK)
        src_row = src[pl.ds(b, 1), :]
        dst_row = dst[pl.ds(b, 1), :]
        edge = mm(pick(column(dst_row), count), sum_grad[...]) * slope[at, :].astype(F32)
        edge = edge.astype(BF)
        acc[...] += mm(spread(src_row, count), edge)
        into[...] += mm(spread(jnp.where(src_row < count, dst_row, -1), count), edge)

    entry[...] = acc[...].astype(BF)


def layer_back_kernel(entry, into, latent_grad, cols, rows, src_w, next_w, update, scale, h_slope, *refs, where, first):
    returned = refs[:NEIGHBOURS]
    outs = refs[NEIGHBOURS:]
    count = entry.shape[0]
    keep = returned[0].shape[0] - 8
    order = SWAP if keep else range(NEIGHBOURS)
    parts = [returned[k][...].astype(F32)[keep:] for k in order]
    short = jnp.zeros((LANES - 8 * NEIGHBOURS, entry.shape[1]), F32)
    back = jnp.concatenate(parts + [short], axis=0).astype(BF)
    row_grad = entry[...].astype(F32) + mm(spread(rows[4][0:1, :], count), back)
    grad = latent_grad[...] + into[...]
    grad += mm_back(row_grad.astype(BF), weight(src_w, where[0], 512))
    step = norm_grad(grad, update[...], scale[:, 0:1])
    summed = mm_back(step, weight(next_w, where[1], 512)).astype(BF)
    if first:
        sum_grad, sends = outs[0], outs[1:]
        which = 0
    else:
        outs[0][...] = grad
        sum_grad, sends = outs[1], outs[2:]
        which = 1
    sum_grad[...] = summed
    put_rows(sends, outgoing_grad(summed, cols[which], h_slope, count).astype(F32))


def encode_back_kernel(sum_grad, slope, src, src_line, dst, entry, edge):
    count = sum_grad.shape[0]

    @pl.loop(0, src.shape[0])
    def _(b):
        at = pl.ds(pl.multiple_of(b * BLOCK, BLOCK), BLOCK)
        grad = mm(pick(column(dst[pl.ds(b, 1), :]), count), sum_grad[...])
        edge[at, :] = (grad * slope[at, :].astype(F32)).astype(BF)

    @pl.loop(0, entry.shape[0] // BLOCK)
    def _(b):
        at = pl.ds(pl.multiple_of(b * BLOCK, BLOCK), BLOCK)
        entry[at, :] = mm(spread(src_line[...] - b * BLOCK, BLOCK), edge[...]).astype(BF)


def input_kernel(entry, skip, slope, rows, w, *refs):
    returned = refs[:NEIGHBOURS]
    out = refs[NEIGHBOURS]
    f_in = out.shape[1]
    embed = weight(w, 0, f_in)
    mix = weight(w, 480, 512)
    back = stack_rows(returned)

    @pl.loop(0, entry.shape[0] // BLOCK)
    def _(b):
        at = pl.ds(pl.multiple_of(b * BLOCK, BLOCK), BLOCK)
        place = spread(rows[3][0:1, :] - b * BLOCK, BLOCK)
        row_grad = (entry[at, :].astype(F32) + mm(place, back)).astype(BF)
        grad = mm_back(row_grad, mix) + skip[at, :]
        grad = (grad * slope[at, :].astype(F32)).astype(BF)
        out[at, :] = mm_back(grad, embed).astype(BF)


def slot_entries(sizes, order):
    table = np.full((8, LANES), -1, np.int32)
    for row, (own, used, apart) in enumerate(sizes):
        for place, k in enumerate(order):
            table[row, place * apart : place * apart + used] = own + k * used + np.arange(used)
    return table


def slot_moves(order):
    shifts = [16 * order.index(k) - 12 * k for k in range(NEIGHBOURS)]
    return np.diff(np.array([0] + shifts)).astype(np.int32)


def permuted(block, route):
    return lax.ppermute(block, "dom", [(i, route(i) % lax.axis_size("dom")) for i in range(lax.axis_size("dom"))])


def exchange(groups, sign):
    each = groups[0].shape[0]
    beside = permuted(jnp.concatenate(groups[:3], axis=0), lambda i: i ^ 1)
    far = permuted(groups[3], lambda i: i + 3 if i % 2 else i - 3)
    up = permuted(jnp.concatenate([beside[each : 2 * each], groups[4]], axis=0), lambda i: i + 2 * sign)
    down = permuted(jnp.concatenate([beside[2 * each :], groups[5]], axis=0), lambda i: i - 2 * sign)
    return [beside[:each], up[:each], down[:each], far, up[each:], down[each:]]


def forward(groups):
    return exchange(groups, 1)


def backward(groups):
    return exchange(groups, -1)


def per_device(
    grid_in,
    mesh_static,
    embed_w,
    grid_w,
    enc_w,
    src_w,
    node_w,
    dec_w,
    out_w,
    cotangent,
    grid_send,
    g2m_src,
    g2m_dst,
    mesh_send,
    mesh_src,
    mesh_dst,
    dec_send,
    m2g_src,
    m2g_dst,
):
    x = grid_in[0]
    cot = cotangent[0]
    grid, f_in = x.shape
    mesh, d = mesh_static.shape
    f_out = cot.shape[1]
    out_pad = jnp.pad(out_w, ((0, 0), (0, 2 * LANES - f_out)))
    first = jnp.concatenate(
        [jnp.pad(embed_w, ((0, 480 - f_in), (0, 0))), grid_w, out_pad[:, :LANES], out_pad[:, LANES:]],
        axis=0,
    )
    w_first = lax.all_gather(first, "phase")
    w_enc = lax.all_gather(jnp.concatenate([enc_w, src_w[0]], axis=0), "phase")
    w_one = lax.all_gather(jnp.concatenate([node_w[0], src_w[1]], axis=0), "phase")
    w_two = lax.all_gather(jnp.concatenate([node_w[1], dec_w], axis=0), "phase")

    gs, gd = g2m_src.reshape(-1, BLOCK), g2m_dst.reshape(-1, BLOCK)
    ms, md = mesh_src.reshape(-1, BLOCK), mesh_dst.reshape(-1, BLOCK)
    ds, dd = m2g_src.reshape(-1, BLOCK), m2g_dst.reshape(-1, BLOCK)
    even = lax.axis_index("dom") % 2 == 0

    def order(table):
        in_even, in_odd = (jnp.stack([table[k] for k in ks]) for ks in (EVEN, ODD))
        return jnp.where(even, in_even, in_odd).reshape(1, -1)

    grid_table = jnp.pad(grid_send[0], ((0, 0), (0, 4)), constant_values=-1)
    tables = [order(grid_table), order(mesh_send[0]), order(dec_send[0])]
    sizes = ((grid, 12, 16), (mesh, 8, 8), (mesh, 8, 8))
    entries = jnp.where(even, slot_entries(sizes, ODD), slot_entries(sizes, EVEN))
    moves = jnp.where(even, slot_moves(ODD), slot_moves(EVEN))
    tables = jnp.concatenate(
        [jnp.pad(t, ((0, 0), (0, LANES - t.shape[1])), constant_values=-1) for t in tables]
        + [jnp.full((5, LANES), -1, jnp.int32)],
        axis=0,
    )
    starts = jnp.minimum(m2g_dst[0, ::HALF] // 16 * 16, grid - BLOCK)
    cols, rows, *sends = call(
        prepare_kernel,
        [jax.ShapeDtypeStruct((6, LANES, LANES), jnp.int32)] * 2 + [shape(32, d)] * 6,
        [gs, gd, ms, md, ds, dd, entries, tables, x, cot],
        400_000_000,
    )
    early = forward(sends)
    slope_in, hidden, ext, own_grad, b_hidden, b_grad = call(
        embed_kernel,
        [shape(grid, d)] * 2 + [shape(grid + LANES, d), shape(grid, d)] + [shape(LANES, d)] * 2,
        [x, cot, w_first, *early],
        1_500_000_000,
    )
    eight = [shape(8, d)] * 6
    enc_slope, enc_far, encoded, enc_scale, latent, proj, *sends = call(
        encode_kernel,
        [shape(gs.size, d), shape(LANES, d), shape(mesh, d, F32), shape(mesh, LANES, F32), shape(mesh, d), shape(mesh, d)]
        + eight,
        [ext, mesh_static, gs, moves, gd, cols, w_enc],
        5_000_000_000,
        [pltpu.VMEM((mesh, d), F32)],
        small=3,
    )
    stored = []
    for layer, w_layer in enumerate((w_one, w_two)):
        halo = forward(sends)
        total, slope = call(
            edges_kernel,
            [shape(mesh, d, F32), shape(ms.size, d)],
            [proj, latent, ms, md],
            3_000_000_000,
        )
        last = layer == 1
        far, update, scale, latent, proj, *sends = call(
            functools.partial(layer_kernel, last=last, starts=(0, d)),
            [shape(LANES, d), shape(mesh, d, F32), shape(mesh, LANES, F32), shape(mesh, d), shape(mesh, d)]
            + ([] if last else eight),
            [total, latent, cols, rows, w_layer, *halo],
            400_000_000,
        )
        stored.append((slope, far, update, scale))

    slope, far, update, scale = stored[1]
    messages, grads, latent_grad, sum_grad, *sends = call(
        functools.partial(decode_kernel, where=(d, 0)),
        [shape(ds.size, d)] * 2 + [shape(mesh, d, F32), shape(mesh, d)] + [shape(16, d)] * 6,
        [proj, hidden, own_grad, b_hidden, b_grad, starts, ds, dd, cols, rows, w_two, w_two, update, scale, far],
        6_000_000_000,
        [pltpu.VMEM((mesh, d), F32)],
        small=5,
    )
    returned = forward(sends)
    halo = returned
    entry, into = call(
        edges_back_kernel,
        [shape(mesh, d), shape(mesh, d, F32)],
        [sum_grad, slope, ms, md, rows, *sends],
        3_000_000_000,
        [pltpu.VMEM((mesh, d), F32)],
    )
    below = stored[0]
    latent_grad, sum_grad, *sends = call(
        functools.partial(layer_back_kernel, where=(d, 0), first=False),
        [shape(mesh, d, F32), shape(mesh, d)] + eight,
        [entry, into, latent_grad, cols, rows, w_one, w_one, below[2], below[3], below[1], *returned],
        400_000_000,
    )
    returned = backward(sends)
    entry, into = call(
        edges_back_kernel,
        [shape(mesh, d), shape(mesh, d, F32)],
        [sum_grad, below[0], ms, md, rows, *sends],
        3_000_000_000,
        [pltpu.VMEM((mesh, d), F32)],
    )
    pred, skip = call(
        predict_kernel,
        [shape(grid, f_out), shape(grid, d, F32)],
        [messages, grads, hidden, own_grad, starts, ds, dd, cols, rows, w_first, *halo],
        5_000_000_000,
        [pltpu.VMEM((grid, d), F32)],
        small=4,
    )
    sum_grad, *sends = call(
        functools.partial(layer_back_kernel, where=(d, 0), first=True),
        [shape(mesh, d)] + [shape(16, d)] * 6,
        [entry, into, latent_grad, cols, rows, w_enc, w_enc, encoded, enc_scale, enc_far, *returned],
        400_000_000,
    )
    returned = backward(sends)
    (entry,) = call(
        encode_back_kernel,
        [shape(grid, d)],
        [sum_grad, enc_slope, gs, g2m_src, gd],
        4_000_000_000,
        [pltpu.VMEM((gs.size, d), BF)],
    )
    (input_grad,) = call(
        input_kernel,
        [shape(grid, f_in)],
        [entry, skip, slope_in, rows, w_first, *returned],
        1_500_000_000,
    )
    return pred[None], input_grad[None]


def solution(mesh):
    placed = (
        P("phase", "dom", None),
        P("dom", None),
        P(None, "phase"),
        P(None, "phase"),
        P(None, "phase"),
        P(None, None, "phase"),
        P(None, None, "phase"),
        P(None, "phase"),
        P("phase", None),
        P("phase", "dom", None),
        P("dom", None, None),
        P("dom", None),
        P("dom", None),
        P("dom", None, None),
        P("dom", None),
        P("dom", None),
        P("dom", None, None),
        P("dom", None),
        P("dom", None),
    )
    return jax.shard_map(
        per_device,
        mesh=mesh,
        in_specs=placed,
        out_specs=(P("phase", "dom", None), P("phase", "dom", None)),
        check_vma=False,
    )
```

```python
import functools

import jax
import jax.numpy as jnp
import numpy as np
from jax import lax
from jax.experimental import pallas as pl
from jax.experimental.pallas import tpu as pltpu
from jax.sharding import PartitionSpec as P

EPSILON = 1e-06
LANES = 128
NEIGHBOURS = 6
BLOCK = 256
HALF = 128
BF = jnp.bfloat16
F32 = jnp.float32
EVEN = (0, 4, 1, 5, 2, 3)
ODD = (1, 0, 5, 4, 2, 3)
SWAP = (0, 2, 1, 3, 5, 4)


def shape(rows, columns, dtype=BF):
    return jax.ShapeDtypeStruct((rows, columns), dtype)


def smem(array):
    return pltpu.SMEM, array


def call(body, outs, args, flops, scratch=(), ties=()):
    outs = [o if isinstance(o, tuple) else (pltpu.VMEM, o) for o in outs]
    args = [a if isinstance(a, tuple) else (pltpu.VMEM, a) for a in args]
    moved = sum(a.size * a.dtype.itemsize for _, a in args)
    moved += sum(o.size * jnp.dtype(o.dtype).itemsize for _, o in outs)

    def kernel(*refs):
        body(*refs[: len(args)], *refs[len(args) + len(ties) :])

    return pl.pallas_call(
        kernel,
        out_shape=tuple(o for _, o in outs),
        in_specs=[pl.BlockSpec(memory_space=m) for m, _ in args]
        + [pl.BlockSpec(memory_space=pl.ANY)] * len(ties),
        out_specs=tuple(pl.BlockSpec(memory_space=m) for m, _ in outs),
        scratch_shapes=list(scratch),
        compiler_params=pltpu.CompilerParams(vmem_limit_bytes=20 << 20),
        cost_estimate=pl.CostEstimate(flops=flops, bytes_accessed=moved, transcendentals=0),
    )(*[a for _, a in args], *ties)


def vmem(rows, columns, dtype=BF):
    return pltpu.VMEM((rows, columns), dtype)


def mm(left, right):
    return jnp.dot(left, right, preferred_element_type=F32)


def mm_back(left, right):
    return lax.dot_general(left, right, (((1,), (1,)), ((), ())), preferred_element_type=F32)


def gate(values):
    return 0.5 * jnp.tanh(0.5 * values) + 0.5


def gate_slope(values, sigmoid):
    return sigmoid * (1.0 + values * (1.0 - sigmoid))


def column(row):
    return jnp.broadcast_to(row, (LANES, row.shape[1])).T


def pick(col, count):
    lane = lax.broadcasted_iota(jnp.int32, col.shape, 1)
    tiles = [
        jnp.where(lane + LANES * t == col, 1.0, 0.0).astype(BF) for t in range(count // LANES)
    ]
    return tiles[0] if len(tiles) == 1 else jnp.concatenate(tiles, axis=1)


def spread(row, count):
    own = lax.broadcasted_iota(jnp.int32, (count, row.shape[1]), 0)
    return jnp.where(own == row, 1.0, 0.0).astype(BF)


def mm_first(left, right):
    return lax.dot_general(left, right, (((0,), (0,)), ((), ())), preferred_element_type=F32)


def section(ref, place):
    return ref[place * 512 : (place + 1) * 512, :]


def assemble(shards, phase, target):
    for away, shard in enumerate(shards):
        block = pl.ds(pl.multiple_of(lax.rem(phase[0] - away + 4, 4) * LANES, LANES), LANES)
        target[:, block] = shard[...]


def at_block(b, size=BLOCK):
    return pl.ds(pl.multiple_of(b * size, size), size)


def line(ref, b, size=BLOCK):
    return ref[:, at_block(b, size)]


def received(refs):
    beside, far, up, down = [r[...].astype(F32) for r in refs]
    each = far.shape[0]
    return [beside[:each], up[:each], down[:each], far, up[each:], down[each:]]


def stacked(groups):
    rows = jnp.concatenate(groups, axis=0)
    short = LANES - rows.shape[0]
    return jnp.concatenate([rows, jnp.zeros((short, rows.shape[1]), F32)], axis=0).astype(BF)


def put(refs, groups):
    beside, far, up, down = refs
    beside[...] = jnp.concatenate(groups[:3], axis=0).astype(BF)
    far[...] = groups[3].astype(BF)
    up[...] = groups[4].astype(BF)
    down[...] = groups[5].astype(BF)


def cut(rows, each):
    return [rows[k * each : (k + 1) * each] for k in range(NEIGHBOURS)]


def inverse_rms(values):
    return lax.rsqrt(jnp.mean(values * values, axis=-1, keepdims=True) + EPSILON)


def norm_grad(grad, update, scale):
    mixed = jnp.mean(grad * update, axis=-1, keepdims=True)
    return (scale * grad - update * (scale * scale * scale) * mixed).astype(BF)


def prepare_kernel(gs, gd, ms, md, ds, dd, dd_small, entries, tables, grid_in, cotangent, cols, rows, starts, *sends):
    last_start = grid_in.shape[1] - HALF - 16
    for b in range(starts.shape[0]):
        starts[b] = jnp.minimum(lax.shift_left(lax.shift_right_logical(dd_small[0, b * HALF], 4), 4), last_start)
    lists = ((gs, gd), (ms, md), (ds, dd))
    for which, (src, dst) in enumerate(lists):
        slots = column(entries[which : which + 1, :])
        entry = jnp.concatenate([slots] * (BLOCK // LANES), axis=1)
        found = jnp.zeros((LANES, BLOCK), F32)
        for b in range(src.shape[1] // BLOCK):
            piece = slice(b * BLOCK, (b + 1) * BLOCK)
            dst_row = jnp.broadcast_to(dst[:, piece], (LANES, BLOCK)).astype(F32)
            found += jnp.where(entry == src[:, piece], dst_row, 0.0)
        total = jnp.sum(found, axis=1, keepdims=True)
        wide = jnp.broadcast_to(total, (LANES, LANES)).astype(jnp.int32)
        wide = jnp.where(slots >= 0, wide, -1)
        cols[which] = wide
        rows[which] = wide.T[:8, :]
    for t in range(3):
        wide = jnp.broadcast_to(tables[t : t + 1, :], (LANES, LANES))
        rows[3 + t] = wide[:8, :]
        cols[3 + t] = wide.T
    count = grid_in.shape[1]
    sent = mm_back(pick(cols[3], count), grid_in[...])
    at = pick(cols[2], count)
    back = mm_back(at, grid_in[...])
    back_cot = mm_back(at, cotangent[...])

    def padded(piece):
        return jnp.concatenate([piece, jnp.zeros((piece.shape[0], 512 - piece.shape[1]), F32)], axis=1)

    groups = []
    for k in range(NEIGHBOURS):
        j = SWAP[k]
        parts = [sent[16 * k : 16 * k + 16], back[8 * j : 8 * j + 8], back_cot[8 * j : 8 * j + 8]]
        groups.append(jnp.concatenate([padded(piece) for piece in parts], axis=0))
    put(sends, groups)


def embed_kernel(grid_in, own, from_1, from_2, from_3, phase, *refs):
    early = refs[:4]
    ext, slope, hidden, b_hidden, b_cot, w = refs[4:]
    f_in, rows = grid_in.shape
    assemble((own, from_1, from_2, from_3), phase, w)
    embed = w[:f_in, :]
    mix = w[480:992, :]
    groups = received(early)
    b_cot[...] = stacked([groups[k][24:32, :256] for k in SWAP])
    pre = mm(stacked([groups[k][16:24, :f_in] for k in SWAP]), embed)
    b_hidden[...] = (pre * gate(pre)).astype(BF)
    pre = mm(stacked([g[:16, :f_in] for g in groups]), embed)
    ext[rows:, :] = mm((pre * gate(pre)).astype(BF), mix).astype(BF)
    size = 512
    for b in range(rows // size):
        at = slice(b * size, (b + 1) * size)
        pre = mm_first(grid_in[:, at], embed)
        sig = gate(pre)
        slope[at, :] = gate_slope(pre, sig).astype(BF)
        own_rows = (pre * sig).astype(BF)
        hidden[at, :] = own_rows
        ext[at, :] = mm(own_rows, mix).astype(BF)


def assemble_kernel(own, from_1, from_2_low, from_2_high, from_3, phase, w):
    half = from_2_low.shape[0]
    low, high = w.at[:half, :], w.at[half:, :]
    assemble((own.at[:half, :], from_1.at[:half, :], from_2_low, from_3.at[:half, :]), phase, low)
    assemble((own.at[half:, :], from_1.at[half:, :], from_2_high, from_3.at[half:, :]), phase, high)


def cotangent_kernel(cotangent, b_cot, w, own_grad, b_grad):
    f_out = cotangent.shape[0]
    out = w[2048 : 2048 + f_out, :]
    own_grad[...] = mm_first(cotangent[...], out).astype(BF)
    b_grad[...] = mm(b_cot[:, :f_out], out).astype(BF)


def encode_edges_kernel(ext, static, src, moves, dst, cols, slope, h_slope, total, messages):
    count = ext.shape[0]
    meshes = static.shape[0]
    pre = ext[count - LANES :, :].astype(F32) + mm(pick(cols[0], meshes), static[...])
    h_slope[...] = gate_slope(pre, gate(pre)).astype(BF)
    size = src.shape[1] // 2
    for b in range(2):
        at = slice(b * size, (b + 1) * size)
        entry = src[:, at]
        src_row = entry
        for k in range(NEIGHBOURS):
            src_row += jnp.where(entry >= count - LANES + 12 * k, moves[k], 0)
        pre = mm(pick(column(src_row), count), ext[...])
        pre += mm(pick(column(dst[:, at]), meshes), static[...])
        sig = gate(pre)
        slope[at, :] = gate_slope(pre, sig).astype(BF)
        messages[at, :] = (pre * sig).astype(BF)
    total[...] = mm(spread(dst[...], meshes), messages[...])


def encode_rows_kernel(total, static, cols, w, *refs):
    encoded, latent, proj = refs[:3]
    made = mm(total[...].astype(BF), w[992:1504, :])
    encoded[...] = made
    start = (static[...].astype(F32) + made * inverse_rms(made)).astype(BF)
    latent[...] = start
    sent = mm(start, w[1504:, :]).astype(BF)
    proj[...] = sent
    put(refs[3:], cut(mm(pick(cols[4], static.shape[0]), sent), 8))


def edges_kernel(proj, latent, src, dst, total, slope, messages):
    count = proj.shape[0]
    size = src.shape[1] // 2
    for b in range(2):
        at = slice(b * size, (b + 1) * size)
        pre = mm(pick(column(src[:, at]), count), proj[...])
        pre += mm(pick(column(dst[:, at]), count), latent[...])
        sig = gate(pre)
        slope[at, :] = gate_slope(pre, sig).astype(BF)
        messages[at, :] = (pre * sig).astype(BF)
    own_row = jnp.where(src[...] < count, dst[...], -1)
    total[...] = mm(spread(own_row, count), messages[...])


def layer_kernel(total, latent, cols, rows, w, *refs, places):
    halo = refs[:4]
    h_slope, update, new, proj = refs[4:8]
    sends = refs[8:]
    count = latent.shape[0]
    old = latent[...]
    pre = stacked(received(halo)).astype(F32) + mm(pick(cols[1], count), old)
    sig = gate(pre)
    h_slope[...] = gate_slope(pre, sig).astype(BF)
    summed = total[...] + mm(spread(rows[1][0:1, :], count), (pre * sig).astype(BF))
    made = mm(summed.astype(BF), section(w, places[0]))
    update[...] = made
    after = (old.astype(F32) + made * inverse_rms(made)).astype(BF)
    new[...] = after
    sent = mm(after, section(w, places[1])).astype(BF)
    proj[...] = sent
    if sends:
        put(sends, cut(mm(pick(cols[4], count), sent), 8))


def outgoing_grad(grad, cols, h_slope, count):
    return (mm(pick(cols, count), grad) * h_slope[...].astype(F32)).astype(BF).astype(F32)


def decode_kernel(proj, hidden, own_grad, b_hidden, b_grad, starts, src, dst, cols, rows, w, update, h_slope, *refs):
    messages, grads, latent_grad, sum_grad = refs[:4]
    sends = refs[4:]
    count = proj.shape[0]
    last_start = hidden.shape[0] - BLOCK

    @pl.loop(0, src.shape[1] // BLOCK, unroll=4)
    def _(b):
        at = at_block(b)
        dst_row = line(dst, b)
        pre = mm(pick(column(line(src, b)), count), proj[...])
        near, grad = [], []
        for half in range(BLOCK // HALF):
            start = pl.multiple_of(jnp.minimum(starts[2 * b + half], last_start), 16)
            window = pl.ds(start, BLOCK)
            chosen = pick(column(dst_row[:, half * HALF : (half + 1) * HALF] - start), BLOCK)
            near.append(mm(chosen, hidden[window, :]))
            grad.append(mm(chosen, own_grad[window, :]))
        pre += jnp.concatenate(near, axis=0)
        sig = gate(pre)
        messages[at, :] = (pre * sig).astype(BF)
        grads[at, :] = (jnp.concatenate(grad, axis=0) * gate_slope(pre, sig)).astype(BF)

    own = mm(spread(src[...], count), grads[...]).astype(BF).astype(F32)
    sent = mm(pick(cols[5], count), proj[...])
    pre = sent + b_hidden[...].astype(F32)
    far = (b_grad[...].astype(F32) * gate_slope(pre, gate(pre))).astype(BF)
    row_grad = (own + mm(spread(rows[5][0:1, :], count), far)).astype(BF)
    grad = mm_back(row_grad, section(w, 3))
    latent_grad[...] = grad
    made = update[...]
    step = norm_grad(grad, made, inverse_rms(made))
    back = mm_back(step, section(w, 2)).astype(BF)
    sum_grad[...] = back
    out = cut(outgoing_grad(back, cols[1], h_slope, count), 8)
    put(sends, [jnp.concatenate([a, out[j]], axis=0) for a, j in zip(cut(sent, 8), SWAP)])


def add_by_row(total, values, starts, src, dst, own):
    rows = HALF + 16

    @pl.loop(0, src.shape[1] // HALF, unroll=4)
    def _(b):
        dst_row = jnp.where(line(src, b, HALF) < own, line(dst, b, HALF), -(1 << 20))
        start = pl.multiple_of(starts[b], 16)
        total[pl.ds(start, rows), :] += mm(spread(dst_row - start, rows), values[at_block(b, HALF), :])


def skip_kernel(grads, hidden, own_grad, starts, src, dst, cols, rows, *refs, own):
    halo = refs[:4]
    skip, message, total = refs[4:]
    count = hidden.shape[0]
    near = pick(cols[2], count)
    far = stacked([g[:8] for g in received(halo)]).astype(F32)
    pre = far + mm(near, hidden[...])
    sig = gate(pre)
    message[...] = (pre * sig).astype(BF)
    edge = (mm(near, own_grad[...]) * gate_slope(pre, sig)).astype(BF)
    total[...] = mm(spread(rows[2][0:1, :], count), edge)
    add_by_row(total, grads, starts, src, dst, own)
    skip[...] = total[...].astype(BF)


def predict_kernel(messages, message, starts, src, dst, rows, w, pred, total, *, own):
    f_out, count = pred.shape
    total[...] = mm(spread(rows[2][0:1, :], count), message[...])
    add_by_row(total, messages, starts, src, dst, own)
    pred[...] = mm_back(w[2048 : 2048 + f_out, :], total[...].astype(BF)).astype(BF)


def edges_back_kernel(sum_grad, slope, src, dst, rows, *refs, both):
    far = refs[:4]
    entry, into, edge = refs[4:]
    count = sum_grad.shape[0]
    size = src.shape[1] // 2
    beside, beyond, up, down = [r[...].astype(F32) for r in far]
    each = beyond.shape[0]
    groups = [beside[k * each : (k + 1) * each] for k in range(3)] + [beyond, up, down]
    if both:
        groups = [groups[k][8:] for k in SWAP]
    for b in range(2):
        at = slice(b * size, (b + 1) * size)
        grad = mm(pick(column(dst[:, at]), count), sum_grad[...])
        edge[at, :] = (grad * slope[at, :].astype(F32)).astype(BF)
    own_row = jnp.where(src[...] < count, dst[...], -1)
    into[...] = mm(spread(rows[1][0:1, :], count), stacked(groups)) + mm(spread(own_row, count), edge[...])
    entry[...] = mm(spread(src[...], count), edge[...]).astype(BF)


def layer_back_kernel(entry, into, latent_grad, cols, rows, src_w, next_w, update, h_slope, *refs, where, both, first):
    groups = received(refs[:4])
    outs = refs[4:]
    count = entry.shape[0]
    if both:
        groups = [groups[k][8:] for k in SWAP]
    row_grad = entry[...].astype(F32) + mm(spread(rows[4][0:1, :], count), stacked(groups))
    grad = latent_grad[...] + into[...] + mm_back(row_grad.astype(BF), src_w[where[0] : where[0] + 512, :])
    made = update[...]
    step = norm_grad(grad, made, inverse_rms(made))
    summed = mm_back(step, next_w[where[1] : where[1] + 512, :]).astype(BF)
    if first:
        sum_grad, sends = outs[0], outs[1:]
    else:
        outs[0][...] = grad
        sum_grad, sends = outs[1], outs[2:]
    sum_grad[...] = summed
    each = sends[1].shape[0]
    put(sends, cut(outgoing_grad(summed, cols[0 if first else 1], h_slope, count), each))


def encode_back_kernel(sum_grad, slope, src, dst, entry, edge):
    count = sum_grad.shape[0]
    size = src.shape[1] // 2
    for b in range(2):
        at = slice(b * size, (b + 1) * size)
        grad = mm(pick(column(dst[:, at]), count), sum_grad[...])
        edge[at, :] = (grad * slope[at, :].astype(F32)).astype(BF)

    @pl.loop(0, entry.shape[0] // BLOCK)
    def _(b):
        entry[at_block(b), :] = mm(spread(src[...] - b * BLOCK, BLOCK), edge[...]).astype(BF)


def input_kernel(entry, w, slope, skip, rows, *refs):
    returned = refs[:4]
    out = refs[4]
    f_in, count = out.shape
    back = stacked(received(returned))
    mix = w[480:992, :]
    size = 512
    for b in range(count // size):
        at = slice(b * size, (b + 1) * size)
        place = spread(rows[3][0:1, :] - b * size, size)
        row_grad = (entry[at, :].astype(F32) + mm(place, back)).astype(BF)
        grad = mm_back(row_grad, mix) + skip[at, :].astype(F32)
        grad = (grad * slope[at, :].astype(F32)).astype(BF)
        out[:, at] = mm_back(w[:f_in, :], grad).astype(BF)


def slot_entries(sizes, order):
    table = np.full((8, LANES), -1, np.int32)
    for row, (own, used, apart) in enumerate(sizes):
        for place, k in enumerate(order):
            table[row, place * apart : place * apart + used] = own + k * used + np.arange(used)
    return table


def slot_moves(order):
    shifts = [16 * order.index(k) - 12 * k for k in range(NEIGHBOURS)]
    return np.diff(np.array([0] + shifts)).astype(np.int32)


def permuted(block, route):
    size = lax.axis_size("dom")
    return lax.ppermute(block, "dom", [(i, route(i) % size) for i in range(size)])


class Exchange:
    def __init__(self, sends, sign):
        beside, far, up, down = sends
        each = far.shape[0]
        self.beside = permuted(beside, lambda i: i ^ 1)
        self.far = permuted(far, lambda i: i + 3 if i % 2 else i - 3)
        up = jnp.concatenate([self.beside[each : 2 * each], up], axis=0)
        down = jnp.concatenate([self.beside[2 * each :], down], axis=0)
        self.ties = (up, down)
        self.up = permuted(up, lambda i: i + 2 * sign)
        self.down = permuted(down, lambda i: i - 2 * sign)

    def rows(self):
        return [self.beside, self.far, self.up, self.down]


def send_shapes(each, d):
    return [shape(3 * each, d)] + [shape(each, d)] * 3


def per_device(
    grid_in,
    mesh_static,
    embed_w,
    grid_w,
    enc_w,
    src_w,
    node_w,
    dec_w,
    out_w,
    cotangent,
    grid_send,
    g2m_src,
    g2m_dst,
    mesh_send,
    mesh_src,
    mesh_dst,
    dec_send,
    m2g_src,
    m2g_dst,
):
    x = grid_in[0].T
    cot = cotangent[0].T
    f_in, grid = x.shape
    mesh, d = mesh_static.shape
    f_out = cot.shape[0]
    edges = mesh_src.size
    phase = lax.axis_index("phase").reshape(1)

    def along(block, away):
        return lax.ppermute(block, "phase", [(i, (i + away) % 4) for i in range(4)])

    w_first = jnp.concatenate([jnp.pad(embed_w, ((0, 480 - f_in), (0, 0))), grid_w, enc_w, src_w[0]], axis=0)
    w_second = jnp.concatenate(
        [src_w[1], node_w[0], node_w[1], dec_w, jnp.pad(out_w.T, ((0, 256 - f_out), (0, 0)))], axis=0
    )
    even = lax.axis_index("dom") % 2 == 0

    def order(table, apart):
        flat = [jnp.pad(table[k], (0, apart - table.shape[1]), constant_values=-1) for k in range(NEIGHBOURS)]
        in_even, in_odd = (jnp.concatenate([flat[k] for k in ks]) for ks in (EVEN, ODD))
        row = jnp.where(even, in_even, in_odd)
        return jnp.pad(row, (0, LANES - row.shape[0]), constant_values=-1)

    tables = [order(grid_send[0], 16), order(mesh_send[0], 8), order(dec_send[0], 8)]
    tables = jnp.stack(tables + [tables[2]] * 5)
    sizes = ((grid, 12, 16), (mesh, 8, 8), (mesh, 8, 8))
    entries = jnp.where(even, slot_entries(sizes, ODD), slot_entries(sizes, EVEN))
    moves = jnp.where(even, slot_moves(ODD), slot_moves(EVEN))
    w_first, w_second, phase, moves, tables = lax.optimization_barrier((w_first, w_second, phase, moves, tables))
    first_1, first_3 = along(w_first, 1), along(w_first, -1)
    first_shards = [w_first, first_1, along(first_1, 1), first_3]
    cols, rows, starts, *sends = call(
        prepare_kernel,
        [
            jax.ShapeDtypeStruct((6, LANES, LANES), jnp.int32),
            jax.ShapeDtypeStruct((6, 8, LANES), jnp.int32),
            smem(jax.ShapeDtypeStruct((m2g_dst.size // HALF,), jnp.int32)),
        ]
        + send_shapes(32, d),
        [g2m_src, g2m_dst, mesh_src, mesh_dst, m2g_src, m2g_dst, smem(m2g_dst), entries, tables, x, cot],
        400_000_000,
        ties=(w_second, phase, moves),
    )
    early = Exchange(sends, 1)
    w_second, _ = lax.optimization_barrier((w_second, early.ties))
    half = w_second.shape[0] // 2
    second_1, second_3 = along(w_second, 1), along(w_second, -1)
    second_2 = (along(second_1[:half], 1), along(second_3[half:], -1))
    ext, slope_in, hidden, b_hidden, b_cot, w_enc = call(
        embed_kernel,
        [shape(grid + LANES, d), shape(grid, d), shape(grid, d), shape(LANES, d), shape(LANES, 256), shape(w_first.shape[0], d)],
        [x, *first_shards, smem(phase), *early.rows()],
        1_500_000_000,
    )
    enc_slope, enc_far, total = call(
        encode_edges_kernel,
        [shape(edges, d), shape(LANES, d), shape(mesh, d, F32)],
        [ext, mesh_static, g2m_src, smem(moves), g2m_dst, cols],
        5_000_000_000,
        [vmem(edges, d)],
        ties=(second_1, second_3),
    )
    encoded, latent, proj, *sends = call(
        encode_rows_kernel,
        [shape(mesh, d, F32), shape(mesh, d), shape(mesh, d)] + send_shapes(8, d),
        [total, mesh_static, cols, w_enc],
        300_000_000,
        ties=second_2,
    )
    stored = []
    for layer in range(2):
        moving = Exchange(sends, 1)
        total, slope = call(
            edges_kernel,
            [shape(mesh, d, F32), shape(edges, d)],
            [proj, latent, mesh_src, mesh_dst],
            3_000_000_000,
            [vmem(edges, d)],
            ties=moving.ties,
        )
        if layer == 0:
            (w,) = call(
                assemble_kernel,
                [shape(w_second.shape[0], d)],
                [w_second, second_1, *second_2, second_3, smem(phase)],
                1_000_000_000,
                ties=moving.ties,
            )
        else:
            own_grad, b_grad = call(
                cotangent_kernel,
                [shape(grid, d), shape(LANES, d)],
                [cot, b_cot, w],
                500_000_000,
                ties=moving.ties,
            )
        far, update, latent, proj, *sends = call(
            functools.partial(layer_kernel, places=(1 + layer, 3 * layer)),
            [shape(LANES, d), shape(mesh, d, F32), shape(mesh, d), shape(mesh, d)]
            + (send_shapes(8, d) if layer == 0 else []),
            [total, latent, cols, rows, w, *moving.rows()],
            400_000_000,
        )
        stored.append((slope, far, update))

    messages, grads, latent_grad, sum_grad, *sends = call(
        decode_kernel,
        [shape(m2g_src.size, d)] * 2 + [shape(mesh, d, F32), shape(mesh, d)] + send_shapes(16, d),
        [proj, hidden, own_grad, b_hidden, b_grad, smem(starts), m2g_src, m2g_dst, cols, rows, w, update, far],
        6_000_000_000,
    )

    def edges_back(sum_grad, slope, sends, both, ties):
        return call(
            functools.partial(edges_back_kernel, both=both),
            [shape(mesh, d), shape(mesh, d, F32)],
            [sum_grad, slope, mesh_src, mesh_dst, rows, *sends],
            3_000_000_000,
            [vmem(edges, d)],
            ties=ties,
        )

    moving = Exchange(sends, 1)
    halo = moving.rows()
    entry, into = edges_back(sum_grad, stored[1][0], sends, True, moving.ties)
    latent_grad, sum_grad, *sends = call(
        functools.partial(layer_back_kernel, where=(0, d), both=True, first=False),
        [shape(mesh, d, F32), shape(mesh, d)] + send_shapes(8, d),
        [entry, into, latent_grad, cols, rows, w, w, stored[0][2], stored[0][1], *halo],
        400_000_000,
    )
    moving = Exchange(sends, -1)
    entry, into = edges_back(sum_grad, stored[0][0], sends, False, moving.ties)
    skip, message = call(
        functools.partial(skip_kernel, own=mesh),
        [shape(grid, d), shape(LANES, d)],
        [grads, hidden, own_grad, smem(starts), m2g_src, m2g_dst, cols, rows, *halo],
        2_500_000_000,
        [vmem(grid, d, F32)],
        ties=moving.ties,
    )
    sum_grad, *sends = call(
        functools.partial(layer_back_kernel, where=(1504, 992), both=False, first=True),
        [shape(mesh, d)] + send_shapes(16, d),
        [entry, into, latent_grad, cols, rows, w_enc, w_enc, encoded, enc_far, *moving.rows()],
        400_000_000,
    )
    moving = Exchange(sends, -1)
    (pred,) = call(
        functools.partial(predict_kernel, own=mesh),
        [shape(f_out, grid)],
        [messages, message, smem(starts), m2g_src, m2g_dst, rows, w],
        2_500_000_000,
        [vmem(grid, d, F32)],
        ties=moving.ties,
    )
    (entry,) = call(
        encode_back_kernel,
        [shape(grid, d)],
        [sum_grad, enc_slope, g2m_src, g2m_dst],
        4_000_000_000,
        [vmem(edges, d)],
        ties=moving.ties,
    )
    (input_grad,) = call(
        input_kernel,
        [shape(f_in, grid)],
        [entry, w_enc, slope_in, skip, rows, *moving.rows()],
        1_500_000_000,
    )
    return pred.T[None], input_grad.T[None]


def solution(mesh):
    placed = (
        P("phase", "dom", None),
        P("dom", None),
        P(None, "phase"),
        P(None, "phase"),
        P(None, "phase"),
        P(None, None, "phase"),
        P(None, None, "phase"),
        P(None, "phase"),
        P("phase", None),
        P("phase", "dom", None),
        P("dom", None, None),
        P("dom", None),
        P("dom", None),
        P("dom", None, None),
        P("dom", None),
        P("dom", None),
        P("dom", None, None),
        P("dom", None),
        P("dom", None),
    )
    return jax.shard_map(
        per_device,
        mesh=mesh,
        in_specs=placed,
        out_specs=(P("phase", "dom", None), P("phase", "dom", None)),
        check_vma=False,
    )
```

```python
import functools

import jax
import jax.numpy as jnp
from jax import lax
from jax.experimental import pallas as pl
from jax.experimental.pallas import tpu as pltpu
from jax.sharding import PartitionSpec as P

EPSILON = 1e-06
LANES = 128
NEIGHBOURS = 6
BLOCK = 256
HALF = 128
BF = jnp.bfloat16
F32 = jnp.float32
EVEN = (0, 4, 1, 5, 2, 3)
ODD = (1, 0, 5, 4, 2, 3)
SWAP = (0, 2, 1, 3, 5, 4)


def shape(rows, columns, dtype=BF):
    return jax.ShapeDtypeStruct((rows, columns), dtype)


def smem(array):
    return pltpu.SMEM, array


def call(body, outs, args, flops, scratch=(), ties=(), limit=20):
    outs = [o if isinstance(o, tuple) else (pltpu.VMEM, o) for o in outs]
    args = [a if isinstance(a, tuple) else (pltpu.VMEM, a) for a in args]
    moved = sum(a.size * a.dtype.itemsize for _, a in args)
    moved += sum(o.size * jnp.dtype(o.dtype).itemsize for _, o in outs)

    def kernel(*refs):
        body(*refs[: len(args)], *refs[len(args) + len(ties) :])

    return pl.pallas_call(
        kernel,
        out_shape=tuple(o for _, o in outs),
        in_specs=[pl.BlockSpec(memory_space=m) for m, _ in args]
        + [pl.BlockSpec(memory_space=pl.ANY)] * len(ties),
        out_specs=tuple(pl.BlockSpec(memory_space=m) for m, _ in outs),
        scratch_shapes=list(scratch),
        compiler_params=pltpu.CompilerParams(vmem_limit_bytes=limit << 20),
        cost_estimate=pl.CostEstimate(flops=flops, bytes_accessed=moved, transcendentals=0),
    )(*[a for _, a in args], *ties)


def vmem(rows, columns, dtype=BF):
    return pltpu.VMEM((rows, columns), dtype)


def mm(left, right):
    return jnp.dot(left, right, preferred_element_type=F32)


def mm_back(left, right):
    return lax.dot_general(left, right, (((1,), (1,)), ((), ())), preferred_element_type=F32)


def gate(values):
    return 0.5 * jnp.tanh(0.5 * values) + 0.5


def gate_slope(values, sigmoid):
    return sigmoid * (1.0 + values * (1.0 - sigmoid))


def column(row):
    return jnp.broadcast_to(row, (LANES, row.shape[1])).T


def pick(col, count):
    lane = lax.broadcasted_iota(jnp.int32, col.shape, 1)
    tiles = [
        jnp.where(lane + LANES * t == col, 1.0, 0.0).astype(BF) for t in range(count // LANES)
    ]
    return tiles[0] if len(tiles) == 1 else jnp.concatenate(tiles, axis=1)


def spread(row, count):
    own = lax.broadcasted_iota(jnp.int32, (count, row.shape[1]), 0)
    return jnp.where(own == row, 1.0, 0.0).astype(BF)


def mm_first(left, right):
    return lax.dot_general(left, right, (((0,), (0,)), ((), ())), preferred_element_type=F32)


def section(ref, place):
    return ref[place * 512 : (place + 1) * 512, :]


def assemble(shards, target):
    phase = lax.axis_index("phase")
    for away, shard in enumerate(shards):
        block = pl.ds(pl.multiple_of(lax.rem(phase - away + 4, 4) * LANES, LANES), LANES)
        target[:, block] = shard[...]


def at_block(b, size=BLOCK):
    return pl.ds(pl.multiple_of(b * size, size), size)


def line(ref, b, size=BLOCK):
    return ref[:, at_block(b, size)]


def received(refs):
    beside, far, up, down = [r[...].astype(F32) for r in refs]
    each = far.shape[0]
    return [beside[:each], up[:each], down[:each], far, up[each:], down[each:]]


def stacked(groups):
    rows = jnp.concatenate(groups, axis=0)
    short = LANES - rows.shape[0]
    return jnp.concatenate([rows, jnp.zeros((short, rows.shape[1]), F32)], axis=0).astype(BF)


def put(refs, groups):
    beside, far, up, down = refs
    beside[...] = jnp.concatenate(groups[:3], axis=0).astype(BF)
    far[...] = groups[3].astype(BF)
    up[...] = groups[4].astype(BF)
    down[...] = groups[5].astype(BF)


def cut(rows, each):
    return [rows[k * each : (k + 1) * each] for k in range(NEIGHBOURS)]


def inverse_rms(values):
    return lax.rsqrt(jnp.mean(values * values, axis=-1, keepdims=True) + EPSILON)


def norm_grad(grad, update, scale):
    mixed = jnp.mean(grad * update, axis=-1, keepdims=True)
    return (scale * grad - update * (scale * scale * scale) * mixed).astype(BF)


def is_even():
    return lax.rem(lax.axis_index("dom"), 2) == 0


def group_at(place, sent):
    mine, other = (EVEN, ODD) if sent else (ODD, EVEN)
    return jnp.where(is_even(), jnp.int32(mine[place]), jnp.int32(other[place]))


def slot_entries(own, used, apart):
    slot = lax.broadcasted_iota(jnp.int32, (LANES, LANES), 0)
    entry = jnp.full((LANES, LANES), -1, jnp.int32)
    for place in range(NEIGHBOURS):
        inner = slot - place * apart
        first = own + group_at(place, False) * used
        entry = jnp.where((inner >= 0) & (inner < used), first + inner, entry)
    return entry


def sent_rows(table, used, apart):
    lane = lax.broadcasted_iota(jnp.int32, (8, LANES), 1)
    row = jnp.full((8, LANES), -1, jnp.int32)
    for place in range(NEIGHBOURS):
        group = group_at(place, True)
        for s in range(used):
            row = jnp.where(lane == place * apart + s, table[group, 0, s], row)
    return row


def prepare_kernel(
    dd_small, grid_send, mesh_send, dec_send,
    grid_in, cotangent, embed_w, out_w,
    g_src, g_dst, m_src, m_dst, d_src, d_dst,
    grid_w, enc_w, src_w, node_w, dec_w,
    cols, rows, starts, w_first, w_second, *refs,
):
    sends, held, sem = refs[:4], refs[4:10], refs[10]
    sources = [g_src, g_dst, m_src, m_dst, d_src, d_dst]
    targets = list(held)
    sources += [grid_w, enc_w, src_w.at[0], src_w.at[1], node_w.at[0], node_w.at[1], dec_w]
    targets += [w_first.at[pl.ds(512 * k + 480, 512), :] for k in range(3)]
    targets += [w_second.at[pl.ds(512 * k, 512), :] for k in range(4)]
    copies = [pltpu.make_async_copy(a, b, sem.at[i]) for i, (a, b) in enumerate(zip(sources, targets))]
    for copy in copies:
        copy.start()
    for copy in copies[: len(held)]:
        copy.wait()
    gs, gd, ms, md, ds, dd = held
    w_first[:480, :] = jnp.concatenate([embed_w[...].astype(F32), jnp.zeros((480 - embed_w.shape[0], LANES), F32)], axis=0).astype(BF)
    w_second[2048:, :] = jnp.concatenate([out_w[...].astype(F32), jnp.zeros((256 - out_w.shape[0], LANES), F32)], axis=0).astype(BF)
    lists = ((gs, gd), (ms, md), (ds, dd))
    grid, mesh = grid_in.shape[1], 256
    sizes = ((grid, 12, 16), (mesh, 8, 8), (mesh, 8, 8))
    last_start = grid_in.shape[1] - HALF - 16
    for b in range(starts.shape[0]):
        starts[b] = jnp.minimum(lax.shift_left(lax.shift_right_logical(dd_small[0, b * HALF], 4), 4), last_start)
    for which, (src, dst) in enumerate(lists):
        slots = slot_entries(*sizes[which])
        entry = jnp.concatenate([slots] * (BLOCK // LANES), axis=1)
        found = jnp.zeros((LANES, BLOCK), F32)
        for b in range(src.shape[1] // BLOCK):
            piece = slice(b * BLOCK, (b + 1) * BLOCK)
            dst_row = jnp.broadcast_to(dst[:, piece], (LANES, BLOCK)).astype(F32)
            found += jnp.where(entry == src[:, piece], dst_row, 0.0)
        total = jnp.sum(found, axis=1, keepdims=True)
        wide = jnp.broadcast_to(total, (LANES, LANES)).astype(jnp.int32)
        wide = jnp.where(slots >= 0, wide, -1)
        cols[which] = wide
        rows[which] = wide.T[:8, :]
    for t, table in enumerate((grid_send, mesh_send, dec_send)):
        row = sent_rows(table, *sizes[t][1:])
        rows[3 + t] = row
        cols[3 + t] = column(row[:1, :])
    count = grid_in.shape[1]
    sent = mm_back(pick(cols[3], count), grid_in[...])
    at = pick(cols[2], count)
    back = mm_back(at, grid_in[...])
    back_cot = mm_back(at, cotangent[...])

    def padded(piece):
        return jnp.concatenate([piece, jnp.zeros((piece.shape[0], 512 - piece.shape[1]), F32)], axis=1)

    groups = []
    for k in range(NEIGHBOURS):
        j = SWAP[k]
        parts = [sent[16 * k : 16 * k + 16], back[8 * j : 8 * j + 8], back_cot[8 * j : 8 * j + 8]]
        groups.append(jnp.concatenate([padded(piece) for piece in parts], axis=0))
    put(sends, groups)
    for copy in copies[len(held) :]:
        copy.wait()


def embed_kernel(grid_in, own, from_1, from_2, from_3, *refs):
    early = refs[:4]
    ext, slope, hidden, b_hidden, b_cot, w = refs[4:]
    f_in, rows = grid_in.shape
    assemble((own, from_1, from_2, from_3), w)
    embed = w[:f_in, :]
    mix = w[480:992, :]
    groups = received(early)
    b_cot[...] = stacked([groups[k][24:32, :256] for k in SWAP])
    pre = mm(stacked([groups[k][16:24, :f_in] for k in SWAP]), embed)
    b_hidden[...] = (pre * gate(pre)).astype(BF)
    pre = mm(stacked([g[:16, :f_in] for g in groups]), embed)
    ext[rows:, :] = mm((pre * gate(pre)).astype(BF), mix).astype(BF)
    size = 512
    for b in range(rows // size):
        at = slice(b * size, (b + 1) * size)
        pre = mm_first(grid_in[:, at], embed)
        sig = gate(pre)
        slope[at, :] = gate_slope(pre, sig).astype(BF)
        own_rows = (pre * sig).astype(BF)
        hidden[at, :] = own_rows
        ext[at, :] = mm(own_rows, mix).astype(BF)


def assemble_kernel(own, from_1, from_2_low, from_2_high, from_3, w):
    half = from_2_low.shape[0]
    low, high = w.at[:half, :], w.at[half:, :]
    assemble((own.at[:half, :], from_1.at[:half, :], from_2_low, from_3.at[:half, :]), low)
    assemble((own.at[half:, :], from_1.at[half:, :], from_2_high, from_3.at[half:, :]), high)


def cotangent_kernel(cotangent, b_cot, w, own_grad, b_grad):
    f_out = cotangent.shape[0]
    out = w[2048 : 2048 + f_out, :]
    own_grad[...] = mm_first(cotangent[...], out).astype(BF)
    b_grad[...] = mm(b_cot[:, :f_out], out).astype(BF)


def encode_edges_kernel(ext, static, src, dst, cols, slope, h_slope, total, messages):
    count = ext.shape[0]
    meshes = static.shape[0]
    pre = ext[count - LANES :, :].astype(F32) + mm(pick(cols[0], meshes), static[...])
    h_slope[...] = gate_slope(pre, gate(pre)).astype(BF)
    size = src.shape[1] // 2
    for b in range(2):
        at = slice(b * size, (b + 1) * size)
        entry = src[:, at]
        src_row = entry
        for k in range(NEIGHBOURS):
            to = [16 * order.index(k) - 12 * k for order in (ODD, EVEN)]
            by = jnp.where(is_even(), jnp.int32(to[0]), jnp.int32(to[1]))
            first = count - LANES + 12 * k
            src_row = jnp.where((entry >= first) & (entry < first + 12), entry + by, src_row)
        pre = mm(pick(column(src_row), count), ext[...])
        pre += mm(pick(column(dst[:, at]), meshes), static[...])
        sig = gate(pre)
        slope[at, :] = gate_slope(pre, sig).astype(BF)
        messages[at, :] = (pre * sig).astype(BF)
    total[...] = mm(spread(dst[...], meshes), messages[...])


def encode_rows_kernel(total, static, cols, w, *refs):
    encoded, latent, proj = refs[:3]
    made = mm(total[...].astype(BF), w[992:1504, :])
    encoded[...] = made
    start = (static[...].astype(F32) + made * inverse_rms(made)).astype(BF)
    latent[...] = start
    sent = mm(start, w[1504:, :]).astype(BF)
    proj[...] = sent
    put(refs[3:], cut(mm(pick(cols[4], static.shape[0]), sent), 8))


def edges_kernel(proj, latent, src, dst, total, slope, messages):
    count = proj.shape[0]
    size = src.shape[1] // 2
    for b in range(2):
        at = slice(b * size, (b + 1) * size)
        pre = mm(pick(column(src[:, at]), count), proj[...])
        pre += mm(pick(column(dst[:, at]), count), latent[...])
        sig = gate(pre)
        slope[at, :] = gate_slope(pre, sig).astype(BF)
        messages[at, :] = (pre * sig).astype(BF)
    own_row = jnp.where(src[...] < count, dst[...], -1)
    total[...] = mm(spread(own_row, count), messages[...])


def layer_kernel(total, latent, cols, rows, w, *refs, places):
    halo = refs[:4]
    h_slope, update, new, proj = refs[4:8]
    sends = refs[8:]
    count = latent.shape[0]
    old = latent[...]
    pre = stacked(received(halo)).astype(F32) + mm(pick(cols[1], count), old)
    sig = gate(pre)
    h_slope[...] = gate_slope(pre, sig).astype(BF)
    summed = total[...] + mm(spread(rows[1][0:1, :], count), (pre * sig).astype(BF))
    made = mm(summed.astype(BF), section(w, places[0]))
    update[...] = made
    after = (old.astype(F32) + made * inverse_rms(made)).astype(BF)
    new[...] = after
    sent = mm(after, section(w, places[1])).astype(BF)
    proj[...] = sent
    if sends:
        put(sends, cut(mm(pick(cols[4], count), sent), 8))


def outgoing_grad(grad, cols, h_slope, count):
    return (mm(pick(cols, count), grad) * h_slope[...].astype(F32)).astype(BF).astype(F32)


def decode_kernel(proj, hidden, own_grad, b_hidden, b_grad, starts, src, dst, cols, rows, w, update, h_slope, *refs):
    messages, grads, latent_grad, sum_grad = refs[:4]
    sends = refs[4:]
    count = proj.shape[0]
    last_start = hidden.shape[0] - BLOCK

    @pl.loop(0, src.shape[1] // BLOCK, unroll=4)
    def _(b):
        at = at_block(b)
        dst_row = line(dst, b)
        pre = mm(pick(column(line(src, b)), count), proj[...])
        near, grad = [], []
        for half in range(BLOCK // HALF):
            start = pl.multiple_of(jnp.minimum(starts[2 * b + half], last_start), 16)
            window = pl.ds(start, BLOCK)
            chosen = pick(column(dst_row[:, half * HALF : (half + 1) * HALF] - start), BLOCK)
            near.append(mm(chosen, hidden[window, :]))
            grad.append(mm(chosen, own_grad[window, :]))
        pre += jnp.concatenate(near, axis=0)
        sig = gate(pre)
        messages[at, :] = (pre * sig).astype(BF)
        grads[at, :] = (jnp.concatenate(grad, axis=0) * gate_slope(pre, sig)).astype(BF)

    own = mm(spread(src[...], count), grads[...]).astype(BF).astype(F32)
    sent = mm(pick(cols[5], count), proj[...])
    pre = sent + b_hidden[...].astype(F32)
    far = (b_grad[...].astype(F32) * gate_slope(pre, gate(pre))).astype(BF)
    row_grad = (own + mm(spread(rows[5][0:1, :], count), far)).astype(BF)
    grad = mm_back(row_grad, section(w, 3))
    latent_grad[...] = grad
    made = update[...]
    step = norm_grad(grad, made, inverse_rms(made))
    back = mm_back(step, section(w, 2)).astype(BF)
    sum_grad[...] = back
    out = cut(outgoing_grad(back, cols[1], h_slope, count), 8)
    put(sends, [jnp.concatenate([a, out[j]], axis=0) for a, j in zip(cut(sent, 8), SWAP)])


def add_by_row(total, values, starts, src, dst, own):
    rows = HALF + 16

    @pl.loop(0, src.shape[1] // HALF, unroll=4)
    def _(b):
        dst_row = jnp.where(line(src, b, HALF) < own, line(dst, b, HALF), -(1 << 20))
        start = pl.multiple_of(starts[b], 16)
        total[pl.ds(start, rows), :] += mm(spread(dst_row - start, rows), values[at_block(b, HALF), :])


def skip_kernel(grads, hidden, own_grad, starts, src, dst, cols, rows, *refs, own):
    halo = refs[:4]
    skip, message, total = refs[4:]
    count = hidden.shape[0]
    near = pick(cols[2], count)
    far = stacked([g[:8] for g in received(halo)]).astype(F32)
    pre = far + mm(near, hidden[...])
    sig = gate(pre)
    message[...] = (pre * sig).astype(BF)
    edge = (mm(near, own_grad[...]) * gate_slope(pre, sig)).astype(BF)
    total[...] = mm(spread(rows[2][0:1, :], count), edge)
    add_by_row(total, grads, starts, src, dst, own)
    skip[...] = total[...].astype(BF)


def grid_sum_kernel(messages, starts, src, dst, total, *, own):
    total[...] = jnp.zeros_like(total)
    add_by_row(total, messages, starts, src, dst, own)


def predict_kernel(total, message, rows, w, pred):
    f_out, count = pred.shape
    summed = total[...] + mm(spread(rows[2][0:1, :], count), message[...])
    pred[...] = mm_back(w[2048 : 2048 + f_out, :], summed.astype(BF)).astype(BF)


def edges_back_kernel(sum_grad, slope, src, dst, rows, *refs, both):
    far = refs[:4]
    entry, into, edge = refs[4:]
    count = sum_grad.shape[0]
    size = src.shape[1] // 2
    beside, beyond, up, down = [r[...].astype(F32) for r in far]
    each = beyond.shape[0]
    groups = [beside[k * each : (k + 1) * each] for k in range(3)] + [beyond, up, down]
    if both:
        groups = [groups[k][8:] for k in SWAP]
    for b in range(2):
        at = slice(b * size, (b + 1) * size)
        grad = mm(pick(column(dst[:, at]), count), sum_grad[...])
        edge[at, :] = (grad * slope[at, :].astype(F32)).astype(BF)
    own_row = jnp.where(src[...] < count, dst[...], -1)
    into[...] = mm(spread(rows[1][0:1, :], count), stacked(groups)) + mm(spread(own_row, count), edge[...])
    entry[...] = mm(spread(src[...], count), edge[...]).astype(BF)


def layer_back_kernel(entry, into, latent_grad, cols, rows, src_w, next_w, update, h_slope, *refs, where, both, first):
    groups = received(refs[:4])
    outs = refs[4:]
    count = entry.shape[0]
    if both:
        groups = [groups[k][8:] for k in SWAP]
    row_grad = entry[...].astype(F32) + mm(spread(rows[4][0:1, :], count), stacked(groups))
    grad = latent_grad[...] + into[...] + mm_back(row_grad.astype(BF), src_w[where[0] : where[0] + 512, :])
    made = update[...]
    step = norm_grad(grad, made, inverse_rms(made))
    summed = mm_back(step, next_w[where[1] : where[1] + 512, :]).astype(BF)
    if first:
        sum_grad, sends = outs[0], outs[1:]
    else:
        outs[0][...] = grad
        sum_grad, sends = outs[1], outs[2:]
    sum_grad[...] = summed
    each = sends[1].shape[0]
    put(sends, cut(outgoing_grad(summed, cols[0 if first else 1], h_slope, count), each))


def encode_back_kernel(sum_grad, slope, src, dst, entry, edge):
    count = sum_grad.shape[0]
    size = src.shape[1] // 2
    for b in range(2):
        at = slice(b * size, (b + 1) * size)
        grad = mm(pick(column(dst[:, at]), count), sum_grad[...])
        edge[at, :] = (grad * slope[at, :].astype(F32)).astype(BF)

    @pl.loop(0, entry.shape[0] // BLOCK)
    def _(b):
        entry[at_block(b), :] = mm(spread(src[...] - b * BLOCK, BLOCK), edge[...]).astype(BF)


def input_kernel(entry, w, slope, skip, rows, *refs):
    returned = refs[:4]
    out = refs[4]
    f_in, count = out.shape
    back = stacked(received(returned))
    mix = w[480:992, :]
    size = 512
    for b in range(count // size):
        at = slice(b * size, (b + 1) * size)
        place = spread(rows[3][0:1, :] - b * size, size)
        row_grad = (entry[at, :].astype(F32) + mm(place, back)).astype(BF)
        grad = mm_back(row_grad, mix) + skip[at, :].astype(F32)
        grad = (grad * slope[at, :].astype(F32)).astype(BF)
        out[:, at] = mm_back(w[:f_in, :], grad).astype(BF)


def permuted(block, route):
    size = lax.axis_size("dom")
    return lax.ppermute(block, "dom", [(i, route(i) % size) for i in range(size)])


class Exchange:
    def __init__(self, sends, sign):
        beside, far, up, down = sends
        each = far.shape[0]
        self.beside = permuted(beside, lambda i: i ^ 1)
        self.far = permuted(far, lambda i: i + 3 if i % 2 else i - 3)
        up = jnp.concatenate([self.beside[each : 2 * each], up], axis=0)
        down = jnp.concatenate([self.beside[2 * each :], down], axis=0)
        self.ties = (up, down)
        self.up = permuted(up, lambda i: i + 2 * sign)
        self.down = permuted(down, lambda i: i - 2 * sign)

    def rows(self):
        return [self.beside, self.far, self.up, self.down]


def send_shapes(each, d):
    return [shape(3 * each, d)] + [shape(each, d)] * 3


def per_device(
    grid_in,
    mesh_static,
    embed_w,
    grid_w,
    enc_w,
    src_w,
    node_w,
    dec_w,
    out_w,
    cotangent,
    grid_send,
    g2m_src,
    g2m_dst,
    mesh_send,
    mesh_src,
    mesh_dst,
    dec_send,
    m2g_src,
    m2g_dst,
):
    x = grid_in[0].T
    cot = cotangent[0].T
    f_in, grid = x.shape
    mesh, d = mesh_static.shape
    f_out = cot.shape[0]
    edges = mesh_src.size

    def along(block, away):
        return lax.ppermute(block, "phase", [(i, (i + away) % 4) for i in range(4)])

    lists = (g2m_src, g2m_dst, mesh_src, mesh_dst, m2g_src, m2g_dst)
    far_away = [(pl.ANY, a) for a in lists + (grid_w, enc_w, src_w, node_w, dec_w)]
    cols, rows, starts, w_first, w_second, *sends = call(
        prepare_kernel,
        [
            jax.ShapeDtypeStruct((6, LANES, LANES), jnp.int32),
            jax.ShapeDtypeStruct((6, 8, LANES), jnp.int32),
            smem(jax.ShapeDtypeStruct((m2g_dst.size // HALF,), jnp.int32)),
            shape(2016, LANES),
            shape(2304, LANES),
        ]
        + send_shapes(32, d),
        [smem(m2g_dst)] + [smem(jnp.swapaxes(table, 0, 1)) for table in (grid_send, mesh_send, dec_send)]
        + [x, cot, embed_w, out_w.T]
        + far_away,
        400_000_000,
        [pltpu.VMEM(a.shape, a.dtype) for a in lists] + [pltpu.SemaphoreType.DMA((13,))],
        limit=56,
    )
    first_shards = [w_first] + [along(w_first, away) for away in (1, 2, 3)]
    early = Exchange(sends, 1)
    w_second, _ = lax.optimization_barrier((w_second, early.ties))
    half = w_second.shape[0] // 2
    second_1, second_3 = along(w_second, 1), along(w_second, -1)
    second_2 = (along(second_1[:half], 1), along(second_3[half:], -1))
    ext, slope_in, hidden, b_hidden, b_cot, w_enc = call(
        embed_kernel,
        [shape(grid + LANES, d), shape(grid, d), shape(grid, d), shape(LANES, d), shape(LANES, 256), shape(w_first.shape[0], d)],
        [x, *first_shards, *early.rows()],
        1_500_000_000,
    )
    enc_slope, enc_far, total = call(
        encode_edges_kernel,
        [shape(edges, d), shape(LANES, d), shape(mesh, d, F32)],
        [ext, mesh_static, g2m_src, g2m_dst, cols],
        5_000_000_000,
        [vmem(edges, d)],
    )
    encoded, latent, proj, *sends = call(
        encode_rows_kernel,
        [shape(mesh, d, F32), shape(mesh, d), shape(mesh, d)] + send_shapes(8, d),
        [total, mesh_static, cols, w_enc],
        300_000_000,
        ties=(second_1, second_3),
    )
    stored = []
    for layer in range(2):
        moving = Exchange(sends, 1)
        total, slope = call(
            edges_kernel,
            [shape(mesh, d, F32), shape(edges, d)],
            [proj, latent, mesh_src, mesh_dst],
            3_000_000_000,
            [vmem(edges, d)],
            ties=moving.ties,
        )
        if layer == 0:
            (w,) = call(
                assemble_kernel,
                [shape(w_second.shape[0], d)],
                [w_second, second_1, *second_2, second_3],
                1_000_000_000,
                ties=moving.ties,
            )
        else:
            own_grad, b_grad = call(
                cotangent_kernel,
                [shape(grid, d), shape(LANES, d)],
                [cot, b_cot, w],
                500_000_000,
                ties=moving.ties,
            )
        far, update, latent, proj, *sends = call(
            functools.partial(layer_kernel, places=(1 + layer, 3 * layer)),
            [shape(LANES, d), shape(mesh, d, F32), shape(mesh, d), shape(mesh, d)]
            + (send_shapes(8, d) if layer == 0 else []),
            [total, latent, cols, rows, w, *moving.rows()],
            400_000_000,
        )
        stored.append((slope, far, update))

    messages, grads, latent_grad, sum_grad, *sends = call(
        decode_kernel,
        [shape(m2g_src.size, d)] * 2 + [shape(mesh, d, F32), shape(mesh, d)] + send_shapes(16, d),
        [proj, hidden, own_grad, b_hidden, b_grad, smem(starts), m2g_src, m2g_dst, cols, rows, w, update, far],
        6_000_000_000,
    )

    def edges_back(sum_grad, slope, sends, both, ties):
        return call(
            functools.partial(edges_back_kernel, both=both),
            [shape(mesh, d), shape(mesh, d, F32)],
            [sum_grad, slope, mesh_src, mesh_dst, rows, *sends],
            3_000_000_000,
            [vmem(edges, d)],
            ties=ties,
        )

    moving = Exchange(sends, 1)
    halo = moving.rows()
    entry, into = edges_back(sum_grad, stored[1][0], sends, True, moving.ties)
    (dec_total,) = call(
        functools.partial(grid_sum_kernel, own=mesh),
        [shape(grid, d, F32)],
        [messages, smem(starts), m2g_src, m2g_dst],
        2_000_000_000,
        ties=moving.ties,
    )
    latent_grad, sum_grad, *sends = call(
        functools.partial(layer_back_kernel, where=(0, d), both=True, first=False),
        [shape(mesh, d, F32), shape(mesh, d)] + send_shapes(8, d),
        [entry, into, latent_grad, cols, rows, w, w, stored[0][2], stored[0][1], *halo],
        400_000_000,
        ties=(dec_total,),
    )
    moving = Exchange(sends, -1)
    entry, into = edges_back(sum_grad, stored[0][0], sends, False, moving.ties)
    skip, message = call(
        functools.partial(skip_kernel, own=mesh),
        [shape(grid, d), shape(LANES, d)],
        [grads, hidden, own_grad, smem(starts), m2g_src, m2g_dst, cols, rows, *halo],
        2_500_000_000,
        [vmem(grid, d, F32)],
        ties=moving.ties,
    )
    sum_grad, *sends = call(
        functools.partial(layer_back_kernel, where=(1504, 992), both=False, first=True),
        [shape(mesh, d)] + send_shapes(16, d),
        [entry, into, latent_grad, cols, rows, w_enc, w_enc, encoded, enc_far, *moving.rows()],
        400_000_000,
        ties=(skip,),
    )
    moving = Exchange(sends, -1)
    (pred,) = call(
        predict_kernel,
        [shape(f_out, grid)],
        [dec_total, message, rows, w],
        500_000_000,
        ties=moving.ties,
    )
    (entry,) = call(
        encode_back_kernel,
        [shape(grid, d)],
        [sum_grad, enc_slope, g2m_src, g2m_dst],
        4_000_000_000,
        [vmem(edges, d)],
        ties=moving.ties,
    )
    (input_grad,) = call(
        input_kernel,
        [shape(f_in, grid)],
        [entry, w_enc, slope_in, skip, rows, *moving.rows()],
        1_500_000_000,
    )
    return pred.T[None], input_grad.T[None]


def solution(mesh):
    placed = (
        P("phase", "dom", None),
        P("dom", None),
        P(None, "phase"),
        P(None, "phase"),
        P(None, "phase"),
        P(None, None, "phase"),
        P(None, None, "phase"),
        P(None, "phase"),
        P("phase", None),
        P("phase", "dom", None),
        P("dom", None, None),
        P("dom", None),
        P("dom", None),
        P("dom", None, None),
        P("dom", None),
        P("dom", None),
        P("dom", None, None),
        P("dom", None),
        P("dom", None),
    )
    return jax.shard_map(
        per_device,
        mesh=mesh,
        in_specs=placed,
        out_specs=(P("phase", "dom", None), P("phase", "dom", None)),
        check_vma=False,
    )
```

```python
import functools

import jax
import jax.numpy as jnp
from jax import lax
from jax.experimental import pallas as pl
from jax.experimental.pallas import tpu as pltpu
from jax.sharding import PartitionSpec as P

EPSILON = 1e-06
LANES = 128
NEIGHBOURS = 6
BLOCK = 256
HALF = 128
BF = jnp.bfloat16
F32 = jnp.float32
EVEN = (0, 4, 1, 5, 2, 3)
ODD = (1, 0, 5, 4, 2, 3)
SWAP = (0, 2, 1, 3, 5, 4)


def shape(rows, columns, dtype=BF):
    return jax.ShapeDtypeStruct((rows, columns), dtype)


def smem(array):
    return pltpu.SMEM, array


def call(body, outs, args, flops, scratch=(), ties=(), limit=20):
    outs = [o if isinstance(o, tuple) else (pltpu.VMEM, o) for o in outs]
    args = [a if isinstance(a, tuple) else (pltpu.VMEM, a) for a in args]
    moved = sum(a.size * a.dtype.itemsize for _, a in args)
    moved += sum(o.size * jnp.dtype(o.dtype).itemsize for _, o in outs)

    def kernel(*refs):
        body(*refs[: len(args)], *refs[len(args) + len(ties) :])

    return pl.pallas_call(
        kernel,
        out_shape=tuple(o for _, o in outs),
        in_specs=[pl.BlockSpec(memory_space=m) for m, _ in args]
        + [pl.BlockSpec(memory_space=pl.ANY)] * len(ties),
        out_specs=tuple(pl.BlockSpec(memory_space=m) for m, _ in outs),
        scratch_shapes=list(scratch),
        compiler_params=pltpu.CompilerParams(vmem_limit_bytes=limit << 20),
        cost_estimate=pl.CostEstimate(flops=flops, bytes_accessed=moved, transcendentals=0),
    )(*[a for _, a in args], *ties)


def vmem(rows, columns, dtype=BF):
    return pltpu.VMEM((rows, columns), dtype)


def mm(left, right):
    return jnp.dot(left, right, preferred_element_type=F32)


def mm_back(left, right):
    return lax.dot_general(left, right, (((1,), (1,)), ((), ())), preferred_element_type=F32)


def gate(values):
    return 0.5 * jnp.tanh(0.5 * values) + 0.5


def gate_slope(values, sigmoid):
    return sigmoid * (1.0 + values * (1.0 - sigmoid))


def column(row):
    return jnp.broadcast_to(row, (LANES, row.shape[1])).T


def pick(col, count):
    lane = lax.broadcasted_iota(jnp.int32, col.shape, 1)
    tiles = [
        jnp.where(lane + LANES * t == col, 1.0, 0.0).astype(BF) for t in range(count // LANES)
    ]
    return tiles[0] if len(tiles) == 1 else jnp.concatenate(tiles, axis=1)


def spread(row, count):
    own = lax.broadcasted_iota(jnp.int32, (count, row.shape[1]), 0)
    return jnp.where(own == row, 1.0, 0.0).astype(BF)


def mm_first(left, right):
    return lax.dot_general(left, right, (((0,), (0,)), ((), ())), preferred_element_type=F32)


def section(ref, place):
    return ref[place * 512 : (place + 1) * 512, :]


def assemble(shards, target):
    phase = lax.axis_index("phase")
    for away, shard in enumerate(shards):
        block = pl.ds(pl.multiple_of(lax.rem(phase - away + 4, 4) * LANES, LANES), LANES)
        target[:, block] = shard[...]


def at_block(b, size=BLOCK):
    return pl.ds(pl.multiple_of(b * size, size), size)


def line(ref, b, size=BLOCK):
    return ref[:, at_block(b, size)]


def received(refs):
    beside, far, up, down = [r[...].astype(F32) for r in refs]
    each = far.shape[0]
    return [beside[:each], up[:each], down[:each], far, up[each:], down[each:]]


def stacked(groups):
    rows = jnp.concatenate(groups, axis=0)
    short = LANES - rows.shape[0]
    return jnp.concatenate([rows, jnp.zeros((short, rows.shape[1]), F32)], axis=0).astype(BF)


def put(refs, groups):
    beside, far, up, down = refs
    beside[...] = jnp.concatenate(groups[:3], axis=0).astype(BF)
    far[...] = groups[3].astype(BF)
    up[...] = groups[4].astype(BF)
    down[...] = groups[5].astype(BF)


def cut(rows, each):
    return [rows[k * each : (k + 1) * each] for k in range(NEIGHBOURS)]


def inverse_rms(values):
    return lax.rsqrt(jnp.mean(values * values, axis=-1, keepdims=True) + EPSILON)


def norm_grad(grad, update, scale):
    mixed = jnp.mean(grad * update, axis=-1, keepdims=True)
    return (scale * grad - update * (scale * scale * scale) * mixed).astype(BF)


def is_even():
    return lax.rem(lax.axis_index("dom"), 2) == 0


def group_at(place, sent):
    mine, other = (EVEN, ODD) if sent else (ODD, EVEN)
    return jnp.where(is_even(), jnp.int32(mine[place]), jnp.int32(other[place]))


def slot_entries(own, used, apart):
    slot = lax.broadcasted_iota(jnp.int32, (LANES, LANES), 0)
    entry = jnp.full((LANES, LANES), -1, jnp.int32)
    for place in range(NEIGHBOURS):
        inner = slot - place * apart
        first = own + group_at(place, False) * used
        entry = jnp.where((inner >= 0) & (inner < used), first + inner, entry)
    return entry


def sent_rows(table, used, apart):
    lane = lax.broadcasted_iota(jnp.int32, (8, LANES), 1)
    row = jnp.full((8, LANES), -1, jnp.int32)
    for place in range(NEIGHBOURS):
        group = group_at(place, True)
        for s in range(used):
            row = jnp.where(lane == place * apart + s, table[group, 0, s], row)
    return row


def pack_kernel(embed_w, out_w, grid_w, enc_w, src_w, node_w, dec_w, w_first, w_second, sem):
    sources = [grid_w, enc_w, src_w.at[0], src_w.at[1], node_w.at[0], node_w.at[1], dec_w]
    targets = [w_first.at[pl.ds(512 * k + 480, 512), :] for k in range(3)]
    targets += [w_second.at[pl.ds(512 * k, 512), :] for k in range(4)]
    copies = [pltpu.make_async_copy(a, b, sem.at[i]) for i, (a, b) in enumerate(zip(sources, targets))]
    for copy in copies:
        copy.start()
    for ref, target in ((embed_w, w_first.at[:480, :]), (out_w, w_second.at[2048:, :])):
        short = target.shape[0] - ref.shape[0]
        target[...] = jnp.concatenate([ref[...].astype(F32), jnp.zeros((short, LANES), F32)], axis=0).astype(BF)
    for copy in copies:
        copy.wait()


def prepare_kernel(
    dd_small, grid_send, mesh_send, dec_send, grid_in, cotangent,
    g_src, g_dst, m_src, m_dst, d_src, d_dst, cols, rows, starts, *refs,
):
    sends, held, sem = refs[:4], refs[4:10], refs[10]
    sources = [g_src, g_dst, m_src, m_dst, d_src, d_dst]
    copies = [pltpu.make_async_copy(a, b, sem.at[i]) for i, (a, b) in enumerate(zip(sources, held))]
    for copy in copies:
        copy.start()
    for copy in copies:
        copy.wait()
    gs, gd, ms, md, ds, dd = held
    lists = ((gs, gd), (ms, md), (ds, dd))
    grid, mesh = grid_in.shape[1], 256
    sizes = ((grid, 12, 16), (mesh, 8, 8), (mesh, 8, 8))
    last_start = grid_in.shape[1] - HALF - 16
    for b in range(starts.shape[0]):
        starts[b] = jnp.minimum(lax.shift_left(lax.shift_right_logical(dd_small[0, b * HALF], 4), 4), last_start)
    for which, (src, dst) in enumerate(lists):
        slots = slot_entries(*sizes[which])
        entry = jnp.concatenate([slots] * (BLOCK // LANES), axis=1)
        found = jnp.zeros((LANES, BLOCK), F32)
        for b in range(src.shape[1] // BLOCK):
            piece = slice(b * BLOCK, (b + 1) * BLOCK)
            dst_row = jnp.broadcast_to(dst[:, piece], (LANES, BLOCK)).astype(F32)
            found += jnp.where(entry == src[:, piece], dst_row, 0.0)
        total = jnp.sum(found, axis=1, keepdims=True)
        wide = jnp.broadcast_to(total, (LANES, LANES)).astype(jnp.int32)
        wide = jnp.where(slots >= 0, wide, -1)
        cols[which] = wide
        rows[which] = wide.T[:8, :]
    for t, table in enumerate((grid_send, mesh_send, dec_send)):
        row = sent_rows(table, *sizes[t][1:])
        rows[3 + t] = row
        cols[3 + t] = column(row[:1, :])
    count = grid_in.shape[1]
    sent = mm_back(pick(cols[3], count), grid_in[...])
    at = pick(cols[2], count)
    back = mm_back(at, grid_in[...])
    back_cot = mm_back(at, cotangent[...])

    def padded(piece):
        return jnp.concatenate([piece, jnp.zeros((piece.shape[0], 512 - piece.shape[1]), F32)], axis=1)

    groups = []
    for k in range(NEIGHBOURS):
        j = SWAP[k]
        parts = [sent[16 * k : 16 * k + 16], back[8 * j : 8 * j + 8], back_cot[8 * j : 8 * j + 8]]
        groups.append(jnp.concatenate([padded(piece) for piece in parts], axis=0))
    put(sends, groups)


def embed_kernel(grid_in, own, from_1, from_2, from_3, *refs):
    early = refs[:4]
    ext, slope, hidden, b_hidden, b_cot, w = refs[4:]
    f_in, rows = grid_in.shape
    assemble((own, from_1, from_2, from_3), w)
    embed = w[:f_in, :]
    mix = w[480:992, :]
    groups = received(early)
    b_cot[...] = stacked([groups[k][24:32, :256] for k in SWAP])
    pre = mm(stacked([groups[k][16:24, :f_in] for k in SWAP]), embed)
    b_hidden[...] = (pre * gate(pre)).astype(BF)
    pre = mm(stacked([g[:16, :f_in] for g in groups]), embed)
    ext[rows:, :] = mm((pre * gate(pre)).astype(BF), mix).astype(BF)
    size = 512
    for b in range(rows // size):
        at = slice(b * size, (b + 1) * size)
        pre = mm_first(grid_in[:, at], embed)
        sig = gate(pre)
        slope[at, :] = gate_slope(pre, sig).astype(BF)
        own_rows = (pre * sig).astype(BF)
        hidden[at, :] = own_rows
        ext[at, :] = mm(own_rows, mix).astype(BF)


def assemble_kernel(own, from_1, from_2_low, from_2_high, from_3, w):
    half = from_2_low.shape[0]
    low, high = w.at[:half, :], w.at[half:, :]
    assemble((own.at[:half, :], from_1.at[:half, :], from_2_low, from_3.at[:half, :]), low)
    assemble((own.at[half:, :], from_1.at[half:, :], from_2_high, from_3.at[half:, :]), high)


def cotangent_kernel(cotangent, b_cot, w, own_grad, b_grad):
    f_out = cotangent.shape[0]
    out = w[2048 : 2048 + f_out, :]
    own_grad[...] = mm_first(cotangent[...], out).astype(BF)
    b_grad[...] = mm(b_cot[:, :f_out], out).astype(BF)


def encode_edges_kernel(ext, static, src, dst, cols, slope, h_slope, total, messages):
    count = ext.shape[0]
    meshes = static.shape[0]
    pre = ext[count - LANES :, :].astype(F32) + mm(pick(cols[0], meshes), static[...])
    h_slope[...] = gate_slope(pre, gate(pre)).astype(BF)
    size = src.shape[1] // 2
    for b in range(2):
        at = slice(b * size, (b + 1) * size)
        entry = src[:, at]
        src_row = entry
        for k in range(NEIGHBOURS):
            to = [16 * order.index(k) - 12 * k for order in (ODD, EVEN)]
            by = jnp.where(is_even(), jnp.int32(to[0]), jnp.int32(to[1]))
            first = count - LANES + 12 * k
            src_row = jnp.where((entry >= first) & (entry < first + 12), entry + by, src_row)
        pre = mm(pick(column(src_row), count), ext[...])
        pre += mm(pick(column(dst[:, at]), meshes), static[...])
        sig = gate(pre)
        slope[at, :] = gate_slope(pre, sig).astype(BF)
        messages[at, :] = (pre * sig).astype(BF)
    total[...] = mm(spread(dst[...], meshes), messages[...])


def encode_rows_kernel(total, static, cols, w, *refs):
    encoded, latent, proj = refs[:3]
    made = mm(total[...].astype(BF), w[992:1504, :])
    encoded[...] = made
    start = (static[...].astype(F32) + made * inverse_rms(made)).astype(BF)
    latent[...] = start
    sent = mm(start, w[1504:, :]).astype(BF)
    proj[...] = sent
    put(refs[3:], cut(mm(pick(cols[4], static.shape[0]), sent), 8))


def edges_kernel(proj, latent, src, dst, total, slope, messages):
    count = proj.shape[0]
    size = src.shape[1] // 2
    for b in range(2):
        at = slice(b * size, (b + 1) * size)
        pre = mm(pick(column(src[:, at]), count), proj[...])
        pre += mm(pick(column(dst[:, at]), count), latent[...])
        sig = gate(pre)
        slope[at, :] = gate_slope(pre, sig).astype(BF)
        messages[at, :] = (pre * sig).astype(BF)
    own_row = jnp.where(src[...] < count, dst[...], -1)
    total[...] = mm(spread(own_row, count), messages[...])


def layer_kernel(total, latent, cols, rows, w, *refs, places):
    halo = refs[:4]
    h_slope, update, new, proj = refs[4:8]
    sends = refs[8:]
    count = latent.shape[0]
    old = latent[...]
    pre = stacked(received(halo)).astype(F32) + mm(pick(cols[1], count), old)
    sig = gate(pre)
    h_slope[...] = gate_slope(pre, sig).astype(BF)
    summed = total[...] + mm(spread(rows[1][0:1, :], count), (pre * sig).astype(BF))
    made = mm(summed.astype(BF), section(w, places[0]))
    update[...] = made
    after = (old.astype(F32) + made * inverse_rms(made)).astype(BF)
    new[...] = after
    sent = mm(after, section(w, places[1])).astype(BF)
    proj[...] = sent
    if sends:
        put(sends, cut(mm(pick(cols[4], count), sent), 8))


def outgoing_grad(grad, cols, h_slope, count):
    return (mm(pick(cols, count), grad) * h_slope[...].astype(F32)).astype(BF).astype(F32)


def decode_kernel(proj, hidden, own_grad, b_hidden, b_grad, starts, src, dst, cols, rows, w, update, h_slope, *refs):
    messages, grads, latent_grad, sum_grad = refs[:4]
    sends = refs[4:]
    count = proj.shape[0]
    last_start = hidden.shape[0] - BLOCK

    @pl.loop(0, src.shape[1] // BLOCK, unroll=6)
    def _(b):
        at = at_block(b)
        dst_row = line(dst, b)
        pre = mm(pick(column(line(src, b)), count), proj[...])
        near, grad = [], []
        for half in range(BLOCK // HALF):
            start = pl.multiple_of(jnp.minimum(starts[2 * b + half], last_start), 16)
            window = pl.ds(start, BLOCK)
            chosen = pick(column(dst_row[:, half * HALF : (half + 1) * HALF] - start), BLOCK)
            near.append(mm(chosen, hidden[window, :]))
            grad.append(mm(chosen, own_grad[window, :]))
        pre += jnp.concatenate(near, axis=0)
        sig = gate(pre)
        messages[at, :] = (pre * sig).astype(BF)
        grads[at, :] = (jnp.concatenate(grad, axis=0) * gate_slope(pre, sig)).astype(BF)

    own = mm(spread(src[...], count), grads[...]).astype(BF).astype(F32)
    sent = mm(pick(cols[5], count), proj[...])
    pre = sent + b_hidden[...].astype(F32)
    far = (b_grad[...].astype(F32) * gate_slope(pre, gate(pre))).astype(BF)
    row_grad = (own + mm(spread(rows[5][0:1, :], count), far)).astype(BF)
    grad = mm_back(row_grad, section(w, 3))
    latent_grad[...] = grad
    made = update[...]
    step = norm_grad(grad, made, inverse_rms(made))
    back = mm_back(step, section(w, 2)).astype(BF)
    sum_grad[...] = back
    out = cut(outgoing_grad(back, cols[1], h_slope, count), 8)
    put(sends, [jnp.concatenate([a, out[j]], axis=0) for a, j in zip(cut(sent, 8), SWAP)])


def add_by_row(total, values, starts, src, dst, own):
    rows = HALF + 16

    @pl.loop(0, src.shape[1] // HALF, unroll=8)
    def _(b):
        dst_row = jnp.where(line(src, b, HALF) < own, line(dst, b, HALF), -(1 << 20))
        start = pl.multiple_of(starts[b], 16)
        total[pl.ds(start, rows), :] += mm(spread(dst_row - start, rows), values[at_block(b, HALF), :])


def skip_kernel(grads, hidden, own_grad, starts, src, dst, cols, rows, *refs, own):
    halo = refs[:4]
    skip, message, total = refs[4:]
    count = hidden.shape[0]
    near = pick(cols[2], count)
    far = stacked([g[:8] for g in received(halo)]).astype(F32)
    pre = far + mm(near, hidden[...])
    sig = gate(pre)
    message[...] = (pre * sig).astype(BF)
    edge = (mm(near, own_grad[...]) * gate_slope(pre, sig)).astype(BF)
    total[...] = mm(spread(rows[2][0:1, :], count), edge)
    add_by_row(total, grads, starts, src, dst, own)
    skip[...] = total[...].astype(BF)


def grid_sum_kernel(messages, starts, src, dst, total, *, own):
    total[...] = jnp.zeros_like(total)
    add_by_row(total, messages, starts, src, dst, own)


def predict_kernel(total, message, rows, w, pred):
    f_out, count = pred.shape
    summed = total[...] + mm(spread(rows[2][0:1, :], count), message[...])
    pred[...] = mm_back(w[2048 : 2048 + f_out, :], summed.astype(BF)).astype(BF)


def edges_back_kernel(sum_grad, slope, src, dst, rows, *refs, both):
    far = refs[:4]
    entry, into, edge = refs[4:]
    count = sum_grad.shape[0]
    size = src.shape[1] // 2
    beside, beyond, up, down = [r[...].astype(F32) for r in far]
    each = beyond.shape[0]
    groups = [beside[k * each : (k + 1) * each] for k in range(3)] + [beyond, up, down]
    if both:
        groups = [groups[k][8:] for k in SWAP]
    for b in range(2):
        at = slice(b * size, (b + 1) * size)
        grad = mm(pick(column(dst[:, at]), count), sum_grad[...])
        edge[at, :] = (grad * slope[at, :].astype(F32)).astype(BF)
    own_row = jnp.where(src[...] < count, dst[...], -1)
    into[...] = mm(spread(rows[1][0:1, :], count), stacked(groups)) + mm(spread(own_row, count), edge[...])
    entry[...] = mm(spread(src[...], count), edge[...]).astype(BF)


def layer_back_kernel(entry, into, latent_grad, cols, rows, src_w, next_w, update, h_slope, *refs, where, both, first):
    groups = received(refs[:4])
    outs = refs[4:]
    count = entry.shape[0]
    if both:
        groups = [groups[k][8:] for k in SWAP]
    row_grad = entry[...].astype(F32) + mm(spread(rows[4][0:1, :], count), stacked(groups))
    grad = latent_grad[...] + into[...] + mm_back(row_grad.astype(BF), src_w[where[0] : where[0] + 512, :])
    made = update[...]
    step = norm_grad(grad, made, inverse_rms(made))
    summed = mm_back(step, next_w[where[1] : where[1] + 512, :]).astype(BF)
    if first:
        sum_grad, sends = outs[0], outs[1:]
    else:
        outs[0][...] = grad
        sum_grad, sends = outs[1], outs[2:]
    sum_grad[...] = summed
    each = sends[1].shape[0]
    put(sends, cut(outgoing_grad(summed, cols[0 if first else 1], h_slope, count), each))


def encode_back_kernel(sum_grad, slope, src, dst, entry, edge):
    count = sum_grad.shape[0]
    size = src.shape[1] // 2
    for b in range(2):
        at = slice(b * size, (b + 1) * size)
        grad = mm(pick(column(dst[:, at]), count), sum_grad[...])
        edge[at, :] = (grad * slope[at, :].astype(F32)).astype(BF)

    @pl.loop(0, entry.shape[0] // BLOCK)
    def _(b):
        entry[at_block(b), :] = mm(spread(src[...] - b * BLOCK, BLOCK), edge[...]).astype(BF)


def input_kernel(entry, w, slope, skip, rows, *refs):
    returned = refs[:4]
    out = refs[4]
    f_in, count = out.shape
    back = stacked(received(returned))
    mix = w[480:992, :]
    size = 512
    for b in range(count // size):
        at = slice(b * size, (b + 1) * size)
        place = spread(rows[3][0:1, :] - b * size, size)
        row_grad = (entry[at, :].astype(F32) + mm(place, back)).astype(BF)
        grad = mm_back(row_grad, mix) + skip[at, :].astype(F32)
        grad = (grad * slope[at, :].astype(F32)).astype(BF)
        out[:, at] = mm_back(w[:f_in, :], grad).astype(BF)


def permuted(block, route):
    size = lax.axis_size("dom")
    return lax.ppermute(block, "dom", [(i, route(i) % size) for i in range(size)])


class Exchange:
    def __init__(self, sends, sign):
        beside, far, up, down = sends
        each = far.shape[0]
        self.beside = permuted(beside, lambda i: i ^ 1)
        self.far = permuted(far, lambda i: i + 3 if i % 2 else i - 3)
        up = jnp.concatenate([self.beside[each : 2 * each], up], axis=0)
        down = jnp.concatenate([self.beside[2 * each :], down], axis=0)
        self.ties = (up, down)
        self.up = permuted(up, lambda i: i + 2 * sign)
        self.down = permuted(down, lambda i: i - 2 * sign)

    def rows(self):
        return [self.beside, self.far, self.up, self.down]


def send_shapes(each, d):
    return [shape(3 * each, d)] + [shape(each, d)] * 3


def per_device(
    grid_in,
    mesh_static,
    embed_w,
    grid_w,
    enc_w,
    src_w,
    node_w,
    dec_w,
    out_w,
    cotangent,
    grid_send,
    g2m_src,
    g2m_dst,
    mesh_send,
    mesh_src,
    mesh_dst,
    dec_send,
    m2g_src,
    m2g_dst,
):
    x = grid_in[0].T
    cot = cotangent[0].T
    f_in, grid = x.shape
    mesh, d = mesh_static.shape
    f_out = cot.shape[0]
    edges = mesh_src.size

    def along(block, away):
        return lax.ppermute(block, "phase", [(i, (i + away) % 4) for i in range(4)])

    lists = (g2m_src, g2m_dst, mesh_src, mesh_dst, m2g_src, m2g_dst)
    w_first, w_second = call(
        pack_kernel,
        [shape(2016, LANES), shape(2304, LANES)],
        [embed_w, out_w.T] + [(pl.ANY, w) for w in (grid_w, enc_w, src_w, node_w, dec_w)],
        1_000_000,
        [pltpu.SemaphoreType.DMA((7,))],
        limit=56,
    )
    first_shards = [w_first] + [along(w_first, away) for away in (1, 2, 3)]
    cols, rows, starts, *sends = call(
        prepare_kernel,
        [
            jax.ShapeDtypeStruct((6, LANES, LANES), jnp.int32),
            jax.ShapeDtypeStruct((6, 8, LANES), jnp.int32),
            smem(jax.ShapeDtypeStruct((m2g_dst.size // HALF,), jnp.int32)),
        ]
        + send_shapes(32, d),
        [smem(m2g_dst)] + [smem(jnp.swapaxes(table, 0, 1)) for table in (grid_send, mesh_send, dec_send)]
        + [x, cot]
        + [(pl.ANY, a) for a in lists],
        400_000_000,
        [pltpu.VMEM(a.shape, a.dtype) for a in lists] + [pltpu.SemaphoreType.DMA((6,))],
        ties=(w_first,),
        limit=56,
    )
    early = Exchange(sends, 1)
    w_second, _ = lax.optimization_barrier((w_second, early.ties))
    half = w_second.shape[0] // 2
    second_1, second_3 = along(w_second, 1), along(w_second, -1)
    second_2 = (along(second_1[:half], 1), along(second_3[half:], -1))
    ext, slope_in, hidden, b_hidden, b_cot, w_enc = call(
        embed_kernel,
        [shape(grid + LANES, d), shape(grid, d), shape(grid, d), shape(LANES, d), shape(LANES, 256), shape(w_first.shape[0], d)],
        [x, *first_shards, *early.rows()],
        1_500_000_000,
    )
    enc_slope, enc_far, total = call(
        encode_edges_kernel,
        [shape(edges, d), shape(LANES, d), shape(mesh, d, F32)],
        [ext, mesh_static, g2m_src, g2m_dst, cols],
        5_000_000_000,
        [vmem(edges, d)],
    )
    encoded, latent, proj, *sends = call(
        encode_rows_kernel,
        [shape(mesh, d, F32), shape(mesh, d), shape(mesh, d)] + send_shapes(8, d),
        [total, mesh_static, cols, w_enc],
        300_000_000,
        ties=(second_1, second_3),
    )
    stored = []
    for layer in range(2):
        moving = Exchange(sends, 1)
        total, slope = call(
            edges_kernel,
            [shape(mesh, d, F32), shape(edges, d)],
            [proj, latent, mesh_src, mesh_dst],
            3_000_000_000,
            [vmem(edges, d)],
            ties=moving.ties,
        )
        if layer == 0:
            (w,) = call(
                assemble_kernel,
                [shape(w_second.shape[0], d)],
                [w_second, second_1, *second_2, second_3],
                1_000_000_000,
                ties=moving.ties,
            )
        else:
            own_grad, b_grad = call(
                cotangent_kernel,
                [shape(grid, d), shape(LANES, d)],
                [cot, b_cot, w],
                500_000_000,
                ties=moving.ties,
            )
        far, update, latent, proj, *sends = call(
            functools.partial(layer_kernel, places=(1 + layer, 3 * layer)),
            [shape(LANES, d), shape(mesh, d, F32), shape(mesh, d), shape(mesh, d)]
            + (send_shapes(8, d) if layer == 0 else []),
            [total, latent, cols, rows, w, *moving.rows()],
            400_000_000,
        )
        stored.append((slope, far, update))

    messages, grads, latent_grad, sum_grad, *sends = call(
        decode_kernel,
        [shape(m2g_src.size, d)] * 2 + [shape(mesh, d, F32), shape(mesh, d)] + send_shapes(16, d),
        [proj, hidden, own_grad, b_hidden, b_grad, smem(starts), m2g_src, m2g_dst, cols, rows, w, update, far],
        6_000_000_000,
    )

    def edges_back(sum_grad, slope, sends, both, ties):
        return call(
            functools.partial(edges_back_kernel, both=both),
            [shape(mesh, d), shape(mesh, d, F32)],
            [sum_grad, slope, mesh_src, mesh_dst, rows, *sends],
            3_000_000_000,
            [vmem(edges, d)],
            ties=ties,
        )

    moving = Exchange(sends, 1)
    halo = moving.rows()
    entry, into = edges_back(sum_grad, stored[1][0], sends, True, moving.ties)
    (dec_total,) = call(
        functools.partial(grid_sum_kernel, own=mesh),
        [shape(grid, d, F32)],
        [messages, smem(starts), m2g_src, m2g_dst],
        2_000_000_000,
        ties=moving.ties,
    )
    latent_grad, sum_grad, *sends = call(
        functools.partial(layer_back_kernel, where=(0, d), both=True, first=False),
        [shape(mesh, d, F32), shape(mesh, d)] + send_shapes(8, d),
        [entry, into, latent_grad, cols, rows, w, w, stored[0][2], stored[0][1], *halo],
        400_000_000,
        ties=(dec_total,),
    )
    moving = Exchange(sends, -1)
    entry, into = edges_back(sum_grad, stored[0][0], sends, False, moving.ties)
    skip, message = call(
        functools.partial(skip_kernel, own=mesh),
        [shape(grid, d), shape(LANES, d)],
        [grads, hidden, own_grad, smem(starts), m2g_src, m2g_dst, cols, rows, *halo],
        2_500_000_000,
        [vmem(grid, d, F32)],
        ties=moving.ties,
    )
    sum_grad, *sends = call(
        functools.partial(layer_back_kernel, where=(1504, 992), both=False, first=True),
        [shape(mesh, d)] + send_shapes(16, d),
        [entry, into, latent_grad, cols, rows, w_enc, w_enc, encoded, enc_far, *moving.rows()],
        400_000_000,
        ties=(skip,),
    )
    moving = Exchange(sends, -1)
    (pred,) = call(
        predict_kernel,
        [shape(f_out, grid)],
        [dec_total, message, rows, w],
        500_000_000,
        ties=moving.ties,
    )
    (entry,) = call(
        encode_back_kernel,
        [shape(grid, d)],
        [sum_grad, enc_slope, g2m_src, g2m_dst],
        4_000_000_000,
        [vmem(edges, d)],
        ties=moving.ties,
    )
    (input_grad,) = call(
        input_kernel,
        [shape(f_in, grid)],
        [entry, w_enc, slope_in, skip, rows, *moving.rows()],
        1_500_000_000,
    )
    return pred.T[None], input_grad.T[None]


def solution(mesh):
    placed = (
        P("phase", "dom", None),
        P("dom", None),
        P(None, "phase"),
        P(None, "phase"),
        P(None, "phase"),
        P(None, None, "phase"),
        P(None, None, "phase"),
        P(None, "phase"),
        P("phase", None),
        P("phase", "dom", None),
        P("dom", None, None),
        P("dom", None),
        P("dom", None),
        P("dom", None, None),
        P("dom", None),
        P("dom", None),
        P("dom", None, None),
        P("dom", None),
        P("dom", None),
    )
    return jax.shard_map(
        per_device,
        mesh=mesh,
        in_specs=placed,
        out_specs=(P("phase", "dom", None), P("phase", "dom", None)),
        check_vma=False,
    )
```

```python
import functools

import jax
import jax.numpy as jnp
from jax import lax
from jax.experimental import pallas as pl
from jax.experimental.pallas import tpu as pltpu
from jax.sharding import PartitionSpec as P

EPSILON = 1e-06
LANES = 128
NEIGHBOURS = 6
BLOCK = 256
HALF = 128
BF = jnp.bfloat16
F32 = jnp.float32
EVEN = (0, 4, 1, 5, 2, 3)
ODD = (1, 0, 5, 4, 2, 3)
SWAP = (0, 2, 1, 3, 5, 4)


def shape(rows, columns, dtype=BF):
    return jax.ShapeDtypeStruct((rows, columns), dtype)


def smem(array):
    return pltpu.SMEM, array


def call(body, outs, args, flops, scratch=(), ties=(), limit=20):
    outs = [o if isinstance(o, tuple) else (pltpu.VMEM, o) for o in outs]
    args = [a if isinstance(a, tuple) else (pltpu.VMEM, a) for a in args]
    moved = sum(a.size * a.dtype.itemsize for _, a in args)
    moved += sum(o.size * jnp.dtype(o.dtype).itemsize for _, o in outs)

    def kernel(*refs):
        body(*refs[: len(args)], *refs[len(args) + len(ties) :])

    return pl.pallas_call(
        kernel,
        out_shape=tuple(o for _, o in outs),
        in_specs=[pl.BlockSpec(memory_space=m) for m, _ in args]
        + [pl.BlockSpec(memory_space=pl.ANY)] * len(ties),
        out_specs=tuple(pl.BlockSpec(memory_space=m) for m, _ in outs),
        scratch_shapes=list(scratch),
        compiler_params=pltpu.CompilerParams(vmem_limit_bytes=limit << 20),
        cost_estimate=pl.CostEstimate(flops=flops, bytes_accessed=moved, transcendentals=0),
    )(*[a for _, a in args], *ties)


def vmem(rows, columns, dtype=BF):
    return pltpu.VMEM((rows, columns), dtype)


def mm(left, right):
    return jnp.dot(left, right, preferred_element_type=F32)


def mm_back(left, right):
    return lax.dot_general(left, right, (((1,), (1,)), ((), ())), preferred_element_type=F32)


def gate(values):
    return 0.5 * jnp.tanh(0.5 * values) + 0.5


def gate_slope(values, sigmoid):
    return sigmoid * (1.0 + values * (1.0 - sigmoid))


def column(row):
    return jnp.broadcast_to(row, (LANES, row.shape[1])).T


def pick(col, count):
    lane = lax.broadcasted_iota(jnp.int32, col.shape, 1)
    tiles = [
        jnp.where(lane + LANES * t == col, 1.0, 0.0).astype(BF) for t in range(count // LANES)
    ]
    return tiles[0] if len(tiles) == 1 else jnp.concatenate(tiles, axis=1)


def spread(row, count):
    own = lax.broadcasted_iota(jnp.int32, (count, row.shape[1]), 0)
    return jnp.where(own == row, 1.0, 0.0).astype(BF)


def mm_first(left, right):
    return lax.dot_general(left, right, (((0,), (0,)), ((), ())), preferred_element_type=F32)


def section(ref, place):
    return ref[place * 512 : (place + 1) * 512, :]


def assemble(shards, target):
    phase = lax.axis_index("phase")
    for away, shard in enumerate(shards):
        block = pl.ds(pl.multiple_of(lax.rem(phase - away + 4, 4) * LANES, LANES), LANES)
        target[:, block] = shard[...]


def at_block(b, size=BLOCK):
    return pl.ds(pl.multiple_of(b * size, size), size)


def line(ref, b, size=BLOCK):
    return ref[:, at_block(b, size)]


def received(refs):
    beside, far, up, down = [r[...].astype(F32) for r in refs]
    each = far.shape[0]
    return [beside[:each], up[:each], down[:each], far, up[each:], down[each:]]


def stacked(groups):
    rows = jnp.concatenate(groups, axis=0)
    short = LANES - rows.shape[0]
    return jnp.concatenate([rows, jnp.zeros((short, rows.shape[1]), F32)], axis=0).astype(BF)


def put(refs, groups):
    beside, far, up, down = refs
    beside[...] = jnp.concatenate(groups[:3], axis=0).astype(BF)
    far[...] = groups[3].astype(BF)
    up[...] = groups[4].astype(BF)
    down[...] = groups[5].astype(BF)


def cut(rows, each):
    return [rows[k * each : (k + 1) * each] for k in range(NEIGHBOURS)]


def inverse_rms(values):
    return lax.rsqrt(jnp.mean(values * values, axis=-1, keepdims=True) + EPSILON)


def norm_grad(grad, update, scale):
    mixed = jnp.mean(grad * update, axis=-1, keepdims=True)
    return (scale * grad - update * (scale * scale * scale) * mixed).astype(BF)


def is_even():
    return lax.rem(lax.axis_index("dom"), 2) == 0


def group_at(place, sent):
    mine, other = (EVEN, ODD) if sent else (ODD, EVEN)
    return jnp.where(is_even(), jnp.int32(mine[place]), jnp.int32(other[place]))


def slot_entries(own, used, apart):
    slot = lax.broadcasted_iota(jnp.int32, (LANES, LANES), 0)
    entry = jnp.full((LANES, LANES), -1, jnp.int32)
    for place in range(NEIGHBOURS):
        inner = slot - place * apart
        first = own + group_at(place, False) * used
        entry = jnp.where((inner >= 0) & (inner < used), first + inner, entry)
    return entry


def sent_rows(table, used, apart):
    lane = lax.broadcasted_iota(jnp.int32, (8, LANES), 1)
    row = jnp.full((8, LANES), -1, jnp.int32)
    for place in range(NEIGHBOURS):
        group = group_at(place, True)
        for s in range(used):
            row = jnp.where(lane == place * apart + s, table[group, 0, s], row)
    return row


def prepare_kernel(
    dd_small, grid_send, mesh_send, dec_send,
    grid_in, cotangent, embed_w, out_w,
    g_src, g_dst, m_src, m_dst, d_src, d_dst,
    grid_w, enc_w, src_w, node_w, dec_w,
    cols, rows, starts, w_first, w_second, *refs,
):
    sends, held, sem = refs[:4], refs[4:10], refs[10]
    sources = [g_src, g_dst, m_src, m_dst, d_src, d_dst]
    targets = list(held)
    sources += [grid_w, enc_w, src_w.at[0], src_w.at[1], node_w.at[0], node_w.at[1], dec_w]
    targets += [w_first.at[pl.ds(512 * k + 480, 512), :] for k in range(3)]
    targets += [w_second.at[pl.ds(512 * k, 512), :] for k in range(4)]
    copies = [pltpu.make_async_copy(a, b, sem.at[i]) for i, (a, b) in enumerate(zip(sources, targets))]
    for copy in copies:
        copy.start()
    for copy in copies[: len(held)]:
        copy.wait()
    gs, gd, ms, md, ds, dd = held
    w_first[:480, :] = jnp.concatenate([embed_w[...].astype(F32), jnp.zeros((480 - embed_w.shape[0], LANES), F32)], axis=0).astype(BF)
    w_second[2048:, :] = jnp.concatenate([out_w[...].astype(F32), jnp.zeros((256 - out_w.shape[0], LANES), F32)], axis=0).astype(BF)
    lists = ((gs, gd), (ms, md), (ds, dd))
    grid, mesh = grid_in.shape[1], 256
    sizes = ((grid, 12, 16), (mesh, 8, 8), (mesh, 8, 8))
    last_start = grid_in.shape[1] - HALF - 16
    for b in range(starts.shape[0]):
        starts[b] = jnp.minimum(lax.shift_left(lax.shift_right_logical(dd_small[0, b * HALF], 4), 4), last_start)
    for which, (src, dst) in enumerate(lists):
        slots = slot_entries(*sizes[which])
        entry = jnp.concatenate([slots] * (BLOCK // LANES), axis=1)
        found = jnp.zeros((LANES, BLOCK), F32)
        for b in range(src.shape[1] // BLOCK):
            piece = slice(b * BLOCK, (b + 1) * BLOCK)
            dst_row = jnp.broadcast_to(dst[:, piece], (LANES, BLOCK)).astype(F32)
            found += jnp.where(entry == src[:, piece], dst_row, 0.0)
        total = jnp.sum(found, axis=1, keepdims=True)
        wide = jnp.broadcast_to(total, (LANES, LANES)).astype(jnp.int32)
        wide = jnp.where(slots >= 0, wide, -1)
        cols[which] = wide
        rows[which] = wide.T[:8, :]
    for t, table in enumerate((grid_send, mesh_send, dec_send)):
        row = sent_rows(table, *sizes[t][1:])
        rows[3 + t] = row
        cols[3 + t] = column(row[:1, :])
    count = grid_in.shape[1]
    sent = mm_back(pick(cols[3], count), grid_in[...])
    at = pick(cols[2], count)
    back = mm_back(at, grid_in[...])
    back_cot = mm_back(at, cotangent[...])

    def padded(piece):
        return jnp.concatenate([piece, jnp.zeros((piece.shape[0], 512 - piece.shape[1]), F32)], axis=1)

    groups = []
    for k in range(NEIGHBOURS):
        j = SWAP[k]
        parts = [sent[16 * k : 16 * k + 16], back[8 * j : 8 * j + 8], back_cot[8 * j : 8 * j + 8]]
        groups.append(jnp.concatenate([padded(piece) for piece in parts], axis=0))
    put(sends, groups)
    for copy in copies[len(held) :]:
        copy.wait()


def embed_kernel(grid_in, own, from_1, from_2, from_3, *refs):
    early = refs[:4]
    ext, slope, hidden, b_hidden, b_cot, w = refs[4:]
    f_in, rows = grid_in.shape
    assemble((own, from_1, from_2, from_3), w)
    embed = w[:f_in, :]
    mix = w[480:992, :]
    groups = received(early)
    b_cot[...] = stacked([groups[k][24:32, :256] for k in SWAP])
    pre = mm(stacked([groups[k][16:24, :f_in] for k in SWAP]), embed)
    b_hidden[...] = (pre * gate(pre)).astype(BF)
    pre = mm(stacked([g[:16, :f_in] for g in groups]), embed)
    ext[rows:, :] = mm((pre * gate(pre)).astype(BF), mix).astype(BF)
    size = 512
    for b in range(rows // size):
        at = slice(b * size, (b + 1) * size)
        pre = mm_first(grid_in[:, at], embed)
        sig = gate(pre)
        slope[at, :] = gate_slope(pre, sig).astype(BF)
        own_rows = (pre * sig).astype(BF)
        hidden[at, :] = own_rows
        ext[at, :] = mm(own_rows, mix).astype(BF)


def assemble_kernel(own, from_1, from_2_low, from_2_high, from_3, w):
    half = from_2_low.shape[0]
    low, high = w.at[:half, :], w.at[half:, :]
    assemble((own.at[:half, :], from_1.at[:half, :], from_2_low, from_3.at[:half, :]), low)
    assemble((own.at[half:, :], from_1.at[half:, :], from_2_high, from_3.at[half:, :]), high)


def cotangent_kernel(cotangent, b_cot, w, own_grad, b_grad):
    f_out = cotangent.shape[0]
    out = w[2048 : 2048 + f_out, :]
    own_grad[...] = mm_first(cotangent[...], out).astype(BF)
    b_grad[...] = mm(b_cot[:, :f_out], out).astype(BF)


def encode_edges_kernel(ext, static, src, dst, cols, slope, h_slope, total, messages):
    count = ext.shape[0]
    meshes = static.shape[0]
    pre = ext[count - LANES :, :].astype(F32) + mm(pick(cols[0], meshes), static[...])
    h_slope[...] = gate_slope(pre, gate(pre)).astype(BF)
    size = src.shape[1] // 2
    for b in range(2):
        at = slice(b * size, (b + 1) * size)
        entry = src[:, at]
        src_row = entry
        for k in range(NEIGHBOURS):
            to = [16 * order.index(k) - 12 * k for order in (ODD, EVEN)]
            by = jnp.where(is_even(), jnp.int32(to[0]), jnp.int32(to[1]))
            first = count - LANES + 12 * k
            src_row = jnp.where((entry >= first) & (entry < first + 12), entry + by, src_row)
        pre = mm(pick(column(src_row), count), ext[...])
        pre += mm(pick(column(dst[:, at]), meshes), static[...])
        sig = gate(pre)
        slope[at, :] = gate_slope(pre, sig).astype(BF)
        messages[at, :] = (pre * sig).astype(BF)
    total[...] = mm(spread(dst[...], meshes), messages[...])


def encode_rows_kernel(total, static, cols, w, *refs):
    encoded, latent, proj = refs[:3]
    made = mm(total[...].astype(BF), w[992:1504, :])
    encoded[...] = made
    start = (static[...].astype(F32) + made * inverse_rms(made)).astype(BF)
    latent[...] = start
    sent = mm(start, w[1504:, :]).astype(BF)
    proj[...] = sent
    put(refs[3:], cut(mm(pick(cols[4], static.shape[0]), sent), 8))


def edges_kernel(proj, latent, src, dst, total, slope, messages):
    count = proj.shape[0]
    size = src.shape[1] // 2
    for b in range(2):
        at = slice(b * size, (b + 1) * size)
        pre = mm(pick(column(src[:, at]), count), proj[...])
        pre += mm(pick(column(dst[:, at]), count), latent[...])
        sig = gate(pre)
        slope[at, :] = gate_slope(pre, sig).astype(BF)
        messages[at, :] = (pre * sig).astype(BF)
    own_row = jnp.where(src[...] < count, dst[...], -1)
    total[...] = mm(spread(own_row, count), messages[...])


def layer_kernel(total, latent, cols, rows, w, *refs, places):
    halo = refs[:4]
    h_slope, update, new, proj = refs[4:8]
    sends = refs[8:]
    count = latent.shape[0]
    old = latent[...]
    pre = stacked(received(halo)).astype(F32) + mm(pick(cols[1], count), old)
    sig = gate(pre)
    h_slope[...] = gate_slope(pre, sig).astype(BF)
    summed = total[...] + mm(spread(rows[1][0:1, :], count), (pre * sig).astype(BF))
    made = mm(summed.astype(BF), section(w, places[0]))
    update[...] = made
    after = (old.astype(F32) + made * inverse_rms(made)).astype(BF)
    new[...] = after
    sent = mm(after, section(w, places[1])).astype(BF)
    proj[...] = sent
    if sends:
        put(sends, cut(mm(pick(cols[4], count), sent), 8))


def outgoing_grad(grad, cols, h_slope, count):
    return (mm(pick(cols, count), grad) * h_slope[...].astype(F32)).astype(BF).astype(F32)


def decode_kernel(proj, hidden, own_grad, b_hidden, b_grad, starts, src, dst, cols, rows, w, update, h_slope, *refs):
    messages, grads, latent_grad, sum_grad = refs[:4]
    sends = refs[4:]
    count = proj.shape[0]
    last_start = hidden.shape[0] - BLOCK

    @pl.loop(0, src.shape[1] // BLOCK, unroll=6)
    def _(b):
        at = at_block(b)
        dst_row = line(dst, b)
        pre = mm(pick(column(line(src, b)), count), proj[...])
        near, grad = [], []
        for half in range(BLOCK // HALF):
            start = pl.multiple_of(jnp.minimum(starts[2 * b + half], last_start), 16)
            window = pl.ds(start, BLOCK)
            chosen = pick(column(dst_row[:, half * HALF : (half + 1) * HALF] - start), BLOCK)
            near.append(mm(chosen, hidden[window, :]))
            grad.append(mm(chosen, own_grad[window, :]))
        pre += jnp.concatenate(near, axis=0)
        sig = gate(pre)
        messages[at, :] = (pre * sig).astype(BF)
        grads[at, :] = (jnp.concatenate(grad, axis=0) * gate_slope(pre, sig)).astype(BF)

    own = mm(spread(src[...], count), grads[...]).astype(BF).astype(F32)
    sent = mm(pick(cols[5], count), proj[...])
    pre = sent + b_hidden[...].astype(F32)
    far = (b_grad[...].astype(F32) * gate_slope(pre, gate(pre))).astype(BF)
    row_grad = (own + mm(spread(rows[5][0:1, :], count), far)).astype(BF)
    grad = mm_back(row_grad, section(w, 3))
    latent_grad[...] = grad
    made = update[...]
    step = norm_grad(grad, made, inverse_rms(made))
    back = mm_back(step, section(w, 2)).astype(BF)
    sum_grad[...] = back
    out = cut(outgoing_grad(back, cols[1], h_slope, count), 8)
    put(sends, [jnp.concatenate([a, out[j]], axis=0) for a, j in zip(cut(sent, 8), SWAP)])


def add_by_row(total, values, starts, src, dst, own):
    rows = HALF + 16

    @pl.loop(0, src.shape[1] // HALF, unroll=8)
    def _(b):
        dst_row = jnp.where(line(src, b, HALF) < own, line(dst, b, HALF), -(1 << 20))
        start = pl.multiple_of(starts[b], 16)
        total[pl.ds(start, rows), :] += mm(spread(dst_row - start, rows), values[at_block(b, HALF), :])


def skip_kernel(grads, hidden, own_grad, starts, src, dst, cols, rows, *refs, own):
    halo = refs[:4]
    skip, message, total = refs[4:]
    count = hidden.shape[0]
    near = pick(cols[2], count)
    far = stacked([g[:8] for g in received(halo)]).astype(F32)
    pre = far + mm(near, hidden[...])
    sig = gate(pre)
    message[...] = (pre * sig).astype(BF)
    edge = (mm(near, own_grad[...]) * gate_slope(pre, sig)).astype(BF)
    total[...] = mm(spread(rows[2][0:1, :], count), edge)
    add_by_row(total, grads, starts, src, dst, own)
    skip[...] = total[...].astype(BF)


def grid_sum_kernel(messages, starts, src, dst, total, *, own):
    total[...] = jnp.zeros_like(total)
    add_by_row(total, messages, starts, src, dst, own)


def predict_kernel(total, message, rows, w, pred):
    f_out, count = pred.shape
    summed = total[...] + mm(spread(rows[2][0:1, :], count), message[...])
    pred[...] = mm_back(w[2048 : 2048 + f_out, :], summed.astype(BF)).astype(BF)


def edges_back_kernel(sum_grad, slope, src, dst, rows, *refs, both):
    far = refs[:4]
    entry, into, edge = refs[4:]
    count = sum_grad.shape[0]
    size = src.shape[1] // 2
    beside, beyond, up, down = [r[...].astype(F32) for r in far]
    each = beyond.shape[0]
    groups = [beside[k * each : (k + 1) * each] for k in range(3)] + [beyond, up, down]
    if both:
        groups = [groups[k][8:] for k in SWAP]
    for b in range(2):
        at = slice(b * size, (b + 1) * size)
        grad = mm(pick(column(dst[:, at]), count), sum_grad[...])
        edge[at, :] = (grad * slope[at, :].astype(F32)).astype(BF)
    own_row = jnp.where(src[...] < count, dst[...], -1)
    into[...] = mm(spread(rows[1][0:1, :], count), stacked(groups)) + mm(spread(own_row, count), edge[...])
    entry[...] = mm(spread(src[...], count), edge[...]).astype(BF)


def layer_back_kernel(entry, into, latent_grad, cols, rows, src_w, next_w, update, h_slope, *refs, where, both, first):
    groups = received(refs[:4])
    outs = refs[4:]
    count = entry.shape[0]
    if both:
        groups = [groups[k][8:] for k in SWAP]
    row_grad = entry[...].astype(F32) + mm(spread(rows[4][0:1, :], count), stacked(groups))
    grad = latent_grad[...] + into[...] + mm_back(row_grad.astype(BF), src_w[where[0] : where[0] + 512, :])
    made = update[...]
    step = norm_grad(grad, made, inverse_rms(made))
    summed = mm_back(step, next_w[where[1] : where[1] + 512, :]).astype(BF)
    if first:
        sum_grad, sends = outs[0], outs[1:]
    else:
        outs[0][...] = grad
        sum_grad, sends = outs[1], outs[2:]
    sum_grad[...] = summed
    each = sends[1].shape[0]
    put(sends, cut(outgoing_grad(summed, cols[0 if first else 1], h_slope, count), each))


def encode_back_kernel(sum_grad, slope, src, dst, entry, edge):
    count = sum_grad.shape[0]
    size = src.shape[1] // 2
    for b in range(2):
        at = slice(b * size, (b + 1) * size)
        grad = mm(pick(column(dst[:, at]), count), sum_grad[...])
        edge[at, :] = (grad * slope[at, :].astype(F32)).astype(BF)

    @pl.loop(0, entry.shape[0] // BLOCK)
    def _(b):
        entry[at_block(b), :] = mm(spread(src[...] - b * BLOCK, BLOCK), edge[...]).astype(BF)


def input_kernel(entry, w, slope, skip, rows, *refs):
    returned = refs[:4]
    out = refs[4]
    f_in, count = out.shape
    back = stacked(received(returned))
    mix = w[480:992, :]
    size = 512
    for b in range(count // size):
        at = slice(b * size, (b + 1) * size)
        place = spread(rows[3][0:1, :] - b * size, size)
        row_grad = (entry[at, :].astype(F32) + mm(place, back)).astype(BF)
        grad = mm_back(row_grad, mix) + skip[at, :].astype(F32)
        grad = (grad * slope[at, :].astype(F32)).astype(BF)
        out[:, at] = mm_back(w[:f_in, :], grad).astype(BF)


def permuted(block, route):
    size = lax.axis_size("dom")
    return lax.ppermute(block, "dom", [(i, route(i) % size) for i in range(size)])


class Exchange:
    def __init__(self, sends, sign):
        beside, far, up, down = sends
        each = far.shape[0]
        self.beside = permuted(beside, lambda i: i ^ 1)
        self.far = permuted(far, lambda i: i + 3 if i % 2 else i - 3)
        up = jnp.concatenate([self.beside[each : 2 * each], up], axis=0)
        down = jnp.concatenate([self.beside[2 * each :], down], axis=0)
        self.ties = (up, down)
        self.up = permuted(up, lambda i: i + 2 * sign)
        self.down = permuted(down, lambda i: i - 2 * sign)

    def rows(self):
        return [self.beside, self.far, self.up, self.down]


def send_shapes(each, d):
    return [shape(3 * each, d)] + [shape(each, d)] * 3


def per_device(
    grid_in,
    mesh_static,
    embed_w,
    grid_w,
    enc_w,
    src_w,
    node_w,
    dec_w,
    out_w,
    cotangent,
    grid_send,
    g2m_src,
    g2m_dst,
    mesh_send,
    mesh_src,
    mesh_dst,
    dec_send,
    m2g_src,
    m2g_dst,
):
    x = grid_in[0].T
    cot = cotangent[0].T
    f_in, grid = x.shape
    mesh, d = mesh_static.shape
    f_out = cot.shape[0]
    edges = mesh_src.size

    def along(block, away):
        return lax.ppermute(block, "phase", [(i, (i + away) % 4) for i in range(4)])

    lists = (g2m_src, g2m_dst, mesh_src, mesh_dst, m2g_src, m2g_dst)
    far_away = [(pl.ANY, a) for a in lists + (grid_w, enc_w, src_w, node_w, dec_w)]
    cols, rows, starts, w_first, w_second, *sends = call(
        prepare_kernel,
        [
            jax.ShapeDtypeStruct((6, LANES, LANES), jnp.int32),
            jax.ShapeDtypeStruct((6, 8, LANES), jnp.int32),
            smem(jax.ShapeDtypeStruct((m2g_dst.size // HALF,), jnp.int32)),
            shape(2016, LANES),
            shape(2304, LANES),
        ]
        + send_shapes(32, d),
        [smem(m2g_dst)] + [smem(jnp.swapaxes(table, 0, 1)) for table in (grid_send, mesh_send, dec_send)]
        + [x, cot, embed_w, out_w.T]
        + far_away,
        400_000_000,
        [pltpu.VMEM(a.shape, a.dtype) for a in lists] + [pltpu.SemaphoreType.DMA((13,))],
        limit=56,
    )
    first_shards = [w_first] + [along(w_first, away) for away in (1, 2, 3)]
    early = Exchange(sends, 1)
    w_second, _ = lax.optimization_barrier((w_second, early.ties))
    half = w_second.shape[0] // 2
    second_1, second_3 = along(w_second, 1), along(w_second, -1)
    second_2 = (along(second_1[:half], 1), along(second_3[half:], -1))
    ext, slope_in, hidden, b_hidden, b_cot, w_enc = call(
        embed_kernel,
        [shape(grid + LANES, d), shape(grid, d), shape(grid, d), shape(LANES, d), shape(LANES, 256), shape(w_first.shape[0], d)],
        [x, *first_shards, *early.rows()],
        1_500_000_000,
    )
    enc_slope, enc_far, total = call(
        encode_edges_kernel,
        [shape(edges, d), shape(LANES, d), shape(mesh, d, F32)],
        [ext, mesh_static, g2m_src, g2m_dst, cols],
        5_000_000_000,
        [vmem(edges, d)],
    )
    encoded, latent, proj, *sends = call(
        encode_rows_kernel,
        [shape(mesh, d, F32), shape(mesh, d), shape(mesh, d)] + send_shapes(8, d),
        [total, mesh_static, cols, w_enc],
        300_000_000,
        ties=(second_1, second_3),
    )
    stored = []
    for layer in range(2):
        moving = Exchange(sends, 1)
        total, slope = call(
            edges_kernel,
            [shape(mesh, d, F32), shape(edges, d)],
            [proj, latent, mesh_src, mesh_dst],
            3_000_000_000,
            [vmem(edges, d)],
            ties=moving.ties,
        )
        if layer == 0:
            (w,) = call(
                assemble_kernel,
                [shape(w_second.shape[0], d)],
                [w_second, second_1, *second_2, second_3],
                1_000_000_000,
                ties=moving.ties,
            )
        else:
            own_grad, b_grad = call(
                cotangent_kernel,
                [shape(grid, d), shape(LANES, d)],
                [cot, b_cot, w],
                500_000_000,
                ties=moving.ties,
            )
        far, update, latent, proj, *sends = call(
            functools.partial(layer_kernel, places=(1 + layer, 3 * layer)),
            [shape(LANES, d), shape(mesh, d, F32), shape(mesh, d), shape(mesh, d)]
            + (send_shapes(8, d) if layer == 0 else []),
            [total, latent, cols, rows, w, *moving.rows()],
            400_000_000,
        )
        stored.append((slope, far, update))

    messages, grads, latent_grad, sum_grad, *sends = call(
        decode_kernel,
        [shape(m2g_src.size, d)] * 2 + [shape(mesh, d, F32), shape(mesh, d)] + send_shapes(16, d),
        [proj, hidden, own_grad, b_hidden, b_grad, smem(starts), m2g_src, m2g_dst, cols, rows, w, update, far],
        6_000_000_000,
    )

    def edges_back(sum_grad, slope, sends, both, ties):
        return call(
            functools.partial(edges_back_kernel, both=both),
            [shape(mesh, d), shape(mesh, d, F32)],
            [sum_grad, slope, mesh_src, mesh_dst, rows, *sends],
            3_000_000_000,
            [vmem(edges, d)],
            ties=ties,
        )

    moving = Exchange(sends, 1)
    halo = moving.rows()
    entry, into = edges_back(sum_grad, stored[1][0], sends, True, moving.ties)
    (dec_total,) = call(
        functools.partial(grid_sum_kernel, own=mesh),
        [shape(grid, d, F32)],
        [messages, smem(starts), m2g_src, m2g_dst],
        2_000_000_000,
        ties=moving.ties,
    )
    latent_grad, sum_grad, *sends = call(
        functools.partial(layer_back_kernel, where=(0, d), both=True, first=False),
        [shape(mesh, d, F32), shape(mesh, d)] + send_shapes(8, d),
        [entry, into, latent_grad, cols, rows, w, w, stored[0][2], stored[0][1], *halo],
        400_000_000,
        ties=(dec_total,),
    )
    moving = Exchange(sends, -1)
    entry, into = edges_back(sum_grad, stored[0][0], sends, False, moving.ties)
    skip, message = call(
        functools.partial(skip_kernel, own=mesh),
        [shape(grid, d), shape(LANES, d)],
        [grads, hidden, own_grad, smem(starts), m2g_src, m2g_dst, cols, rows, *halo],
        2_500_000_000,
        [vmem(grid, d, F32)],
        ties=moving.ties,
    )
    sum_grad, *sends = call(
        functools.partial(layer_back_kernel, where=(1504, 992), both=False, first=True),
        [shape(mesh, d)] + send_shapes(16, d),
        [entry, into, latent_grad, cols, rows, w_enc, w_enc, encoded, enc_far, *moving.rows()],
        400_000_000,
        ties=(skip,),
    )
    moving = Exchange(sends, -1)
    (pred,) = call(
        predict_kernel,
        [shape(f_out, grid)],
        [dec_total, message, rows, w],
        500_000_000,
        ties=moving.ties,
    )
    (entry,) = call(
        encode_back_kernel,
        [shape(grid, d)],
        [sum_grad, enc_slope, g2m_src, g2m_dst],
        4_000_000_000,
        [vmem(edges, d)],
        ties=moving.ties,
    )
    (input_grad,) = call(
        input_kernel,
        [shape(f_in, grid)],
        [entry, w_enc, slope_in, skip, rows, *moving.rows()],
        1_500_000_000,
    )
    return pred.T[None], input_grad.T[None]


def solution(mesh):
    placed = (
        P("phase", "dom", None),
        P("dom", None),
        P(None, "phase"),
        P(None, "phase"),
        P(None, "phase"),
        P(None, None, "phase"),
        P(None, None, "phase"),
        P(None, "phase"),
        P("phase", None),
        P("phase", "dom", None),
        P("dom", None, None),
        P("dom", None),
        P("dom", None),
        P("dom", None, None),
        P("dom", None),
        P("dom", None),
        P("dom", None, None),
        P("dom", None),
        P("dom", None),
    )
    return jax.shard_map(
        per_device,
        mesh=mesh,
        in_specs=placed,
        out_specs=(P("phase", "dom", None), P("phase", "dom", None)),
        check_vma=False,
    )
```
